512 devices in a mesh: chol: 8 (over x, core), walk: 64 (over y, z).
Axes of the slice: x: 4, y: 8, z: 8, core: 2. Of those that a mesh axis runs over, the one named last changes fastest.
Arguments:
- walkers: float32 [256, 200, 768], P('walk'), may hold values from -6 to 6
- inv_intersection: float32 [256, 2, 100, 100], P('walk'), may hold values from -0.625 to 0.625
- half_vectors: bfloat16 [1024, 200, 768], P('chol', None, 'walk'), may hold values from -0.375 to 0.375
- chol_vectors: bfloat16 [1024, 768, 768], P('chol', 'walk'), may hold values from -0.1875 to 0.1875
- field_draw: float32 [256, 1024], P(None, 'chol'), may hold values from -6 to 6
- counts: int32 [256], replicated, may hold values from 0 to 8, as said below
Outputs:
- new_walkers: float32 [256, 200, 768], P('walk', None, 'chol')
The draws below stay inside these ranges and needn't reach their ends.
Inputs may be any that keep to these rules, and one draw needn't show every extreme that they name: In each aligned block of 8 walkers the counts sum to 8.
All inputs are finite; a program needn't handle non-finite values.
Results may differ from the reference program's by a relative error of at most 0.024.
Values may be sent and summed in bfloat16 or wider, within the bound.
A program may use at most 64 MiB of HBM per device.

```python
import jax
import jax.numpy as jnp
from jax import lax

M = 768
NUP = 100
NCHOL = 1024
NE = 200
WALKERS = 256
CHOL_DEV = 128
PAIR_WALKERS = 8
N_CHOL = 8


def draw_counts(key, part):
    key = jax.random.fold_in(key, 7)
    pick_key = jax.random.fold_in(key, 1)
    block_key = jax.random.fold_in(key, 2)
    block_total = WALKERS // PAIR_WALKERS
    pick_index = jax.random.randint(pick_key, (block_total, PAIR_WALKERS), 0, PAIR_WALKERS)
    chosen = jax.random.randint(block_key, (), 0, block_total)
    is_chosen = jnp.arange(block_total, dtype=jnp.int32) == chosen
    pick_index = jnp.where(is_chosen[:, None], pick_index[:, :1], pick_index)
    owners = jnp.arange(PAIR_WALKERS, dtype=jnp.int32)
    tallies = jnp.sum((pick_index[:, :, None] == owners[None, None, :]).astype(jnp.int32), axis=1)
    return tallies.reshape(WALKERS).astype(jnp.int32)


def block_scale(key, dims, pieces, smallest, top_value):
    level, own = 1.0, jax.random.fold_in(key, 6)
    for axis_at, parts in pieces:
        steps = jnp.exp(jax.random.uniform(jax.random.fold_in(own, axis_at), (parts,), jnp.float32, smallest / len(pieces), top_value / len(pieces)))
        level = level * jnp.repeat(steps, dims[axis_at] // parts).reshape([-1 if axis == axis_at else 1 for axis in range(len(dims))])
    return level


def normal_values(own_key, shape, deviation, bound, shards=(), kind=jnp.bfloat16):
    entries = deviation * jax.random.normal(own_key, shape, jnp.float32)
    if shards:
        entries = entries * block_scale(own_key, shape, shards, -0.22, 0.18)
    return jnp.clip(entries, -bound, bound).astype(kind)


def setup_inputs(seed: int = 0) -> dict:
    seeds = jax.random.split(jax.random.key(seed), 7)
    walkers = normal_values(seeds[0], (WALKERS, NE, M), 1.0, 6.0, ((0, 64),), jnp.float32)
    inv_intersection = normal_values(seeds[1], (WALKERS, 2, NUP, NUP), NUP ** -0.5, 0.625, ((0, 64),), jnp.float32)
    half_vectors = normal_values(seeds[2], (NCHOL, NE, M), (10.0 * (NE * M) ** -0.5), 0.375, ((0, 8), (2, 64)))
    chol_vectors = normal_values(seeds[3], (NCHOL, M, M), (10.6 * (NCHOL * M) ** -0.5), 0.1875, ((0, 8), (1, 64)))
    field_draw = normal_values(seeds[4], (WALKERS, NCHOL), 1.0, 6.0, ((1, 8),), jnp.float32)
    counts = draw_counts(jax.random.fold_in(seeds[6], 71), 0)
    return {"walkers": walkers, "inv_intersection": inv_intersection, "half_vectors": half_vectors, "chol_vectors": chol_vectors, "field_draw": field_draw, "counts": counts}


root_step = 0.1


def inverse_apply(inv_intersection, walkers):
    half_count = inv_intersection.shape[-1]
    spin_up = jnp.einsum("wij,wjk->wik", inv_intersection[:, 0], walkers[:, :half_count], precision=lax.Precision.HIGHEST)
    spin_down = jnp.einsum("wij,wjk->wik", inv_intersection[:, 1], walkers[:, half_count:], precision=lax.Precision.HIGHEST)
    return jnp.concatenate([spin_up, spin_down], axis=1)


def reference(walkers, inv_intersection, half_vectors, chol_vectors, field_draw, counts):
    mixed = inverse_apply(inv_intersection, walkers).astype(jnp.bfloat16)
    flat_mixed = mixed.reshape(WALKERS, NE * M)
    flat_half = half_vectors.reshape(NCHOL, NE * M)
    force_bias = root_step * jnp.dot(flat_mixed, flat_half.T, preferred_element_type=jnp.float32)
    shifted = (field_draw + force_bias).astype(jnp.bfloat16)
    summed = jnp.zeros((WALKERS, M * M), jnp.float32)
    for group in range(N_CHOL):
        vectors = chol_vectors[group * CHOL_DEV:(group + 1) * CHOL_DEV].reshape(CHOL_DEV, M * M)
        products = jnp.dot(shifted[:, group * CHOL_DEV:(group + 1) * CHOL_DEV], vectors, preferred_element_type=jnp.float32)
        rounded = lax.optimization_barrier((root_step * products).astype(jnp.bfloat16))
        summed = summed + rounded.astype(jnp.float32)
    field = summed.astype(jnp.bfloat16).reshape(WALKERS, M, M)
    field_wide = field.astype(jnp.float32)
    current = walkers.astype(jnp.bfloat16)
    propagated = walkers
    for degree in range(1, 5):
        taylor_term = jnp.einsum("wel,wkl->wek", current.astype(jnp.float32), field_wide) / degree
        propagated = propagated + taylor_term
        current = taylor_term.astype(jnp.bfloat16)
    cumulative = jnp.cumsum(counts, dtype=jnp.int32)
    slot_index = jnp.arange(WALKERS, dtype=jnp.int32)
    source = jnp.sum((cumulative[None, :] <= slot_index[:, None]).astype(jnp.int32), axis=1)
    return jnp.take(propagated, source, axis=0)
```

```python
import jax
import jax.numpy as jnp
from jax import lax
from jax.experimental import pallas as pl
from jax.experimental.pallas import tpu as pltpu
from jax.sharding import PartitionSpec as P

root_step = 0.1

NX, NY, NZ = 4, 8, 8
LANES = 128
HALF_E = 100
SHIFT = LANES - HALF_E
M = 768
LH = M // 2
KW = M // (NY * NZ)
XI = KW // NX
WALKERS = NX * NY * NZ
GROUP = 128
COPIES = 160
MESH = pl.DeviceIdType.MESH


def kernel(
    walkers, inverse, half, chol, draw, counts, out,
    wbuf, wt, hbuf, hs, hsend, m1, s1, s1f, s2, mx, mbig, fsend, fown, frecv, fz, fr, fy, fyr,
    drawbuf, sg, cr, pz, rz, qx, rx, gbuf, qy, fb, cur, prop, cand, ssem, rsem, lsem,
):
    c = lax.axis_index("chol")
    w = lax.axis_index("walk")
    x = lax.div(c, 2)
    core = lax.rem(c, 2)
    y = lax.div(w, NZ)
    z = lax.rem(w, NZ)
    other = 1 - core
    partner_w = w + 1 - 2 * lax.rem(w, 2)

    def at_y(d):
        t = lax.rem(y + d, NY)
        return t, (c, t * NZ + z)

    def at_z(d):
        t = lax.rem(z + d, NZ)
        return t, (c, y * NZ + t)

    def at_x(d):
        t = lax.rem(x + d, NX)
        return t, (t * 2 + core, w)

    mate = (x * 2 + other, w)

    barrier = pltpu.get_barrier_semaphore()
    greeted = 0
    peers = [at_y(d)[1] for d in range(1, NY)] + [at_z(d)[1] for d in range(1, NZ)]
    finals = []
    for dx in range(NX):
        for dc in range(2):
            tx = lax.rem(x + dx, NX)
            tc = tx * 2 + (core if dc == 0 else other)
            for dp in range(2):
                if dx or dc or dp:
                    finals.append((dx, dc, dp, tc, (tc, partner_w if dp else w)))
                    if dx or dc:
                        peers.append((tc, partner_w if dp else w))
    for peer in peers:
        pl.semaphore_signal(barrier, inc=1, device_id=peer, device_id_type=MESH)
        greeted += 1

    started = []

    def send(src, dst, device):
        i = len(started)
        copy = pltpu.make_async_remote_copy(
            src_ref=src, dst_ref=dst, send_sem=ssem.at[i], recv_sem=rsem.at[i],
            device_id=device, device_id_type=MESH,
        )
        copy.start()
        started.append(copy)
        return copy

    load_w = pltpu.make_async_copy(walkers.at[x], wbuf, lsem.at[0])
    load_h = pltpu.make_async_copy(half, hbuf, lsem.at[1])
    load_d = pltpu.make_async_copy(draw, drawbuf, lsem.at[2])
    load_c = pltpu.make_async_copy(
        chol.at[pl.ds(XI * x, XI), :, pl.ds(pl.multiple_of(LH * core, LANES), LH)], cr.at[c], lsem.at[3]
    )
    load_w.start()
    load_h.start()
    load_d.start()
    load_c.start()

    load_w.wait()
    electron = lax.broadcasted_iota(jnp.int32, (LANES, M), 0)
    up = jnp.where(electron < HALF_E, wbuf[0:LANES, :], 0.0)
    down = jnp.where(electron >= SHIFT, wbuf[2 * HALF_E - LANES : 2 * HALF_E, :], 0.0)
    wt[...] = jnp.where(core == 0, up, down).T
    mixed = lax.dot_general(
        wt[...], inverse[...], (((1,), (1,)), ((), ())),
        precision=lax.Precision.HIGHEST, preferred_element_type=jnp.float32,
    )
    m1[...] = mixed.astype(jnp.bfloat16).reshape(NY, M // NY, LANES)
    s1[y] = m1[y]

    pl.semaphore_wait(barrier, greeted)

    copies = []
    for d in range(1, NY):
        t, device = at_y(d)
        copies.append(send(m1.at[t], s1.at[y], device))

    chol_copies = []
    for dx in range(NX):
        for dc in range(2):
            if dx or dc:
                tx = lax.rem(x + dx, NX)
                tcore = core if dc == 0 else other
                chol_copies.append(
                    send(
                        chol.at[pl.ds(XI * tx, XI), :, pl.ds(pl.multiple_of(LH * tcore, LANES), LH)],
                        cr.at[c],
                        (tx * 2 + tcore, w),
                    )
                )

    load_h.wait()
    for k in range(KW):
        rows = hbuf[k].astype(jnp.float32)
        first = rows[0:LANES]
        second = rows[2 * HALF_E - LANES : 2 * HALF_E]
        hs[core, LANES * k : LANES * (k + 1)] = jnp.where(core == 0, first, second).astype(jnp.bfloat16)
        hsend[LANES * k : LANES * (k + 1)] = jnp.where(core == 0, second, first).astype(jnp.bfloat16)
    half_copy = send(hsend, hs.at[core], mate)

    for copy in copies:
        copy.wait_recv()

    rows_y = M // NY
    for t in range(NY):
        s1f[rows_y * t : rows_y * (t + 1)] = s1[t].astype(jnp.float32)

    @pl.loop(0, NZ)
    def _(t):
        for p in range(KW // 2):
            pair = [s1f[pl.ds(KW * t + 2 * p + q, NY, stride=rows_y), :] for q in range(2)]
            s2[t, 16 * p : 16 * (p + 1)] = jnp.concatenate(pair, axis=0).astype(jnp.bfloat16)

    mx[x, z] = s2[z]
    copies = []
    for d in range(1, NZ):
        t, device = at_z(d)
        copies.append(send(s2.at[t], mx.at[x, z], device))
    for copy in copies:
        copy.wait_recv()

    copies = []
    for d in range(1, NX):
        copies.append(send(mx.at[x], mx.at[x], at_x(d)[1]))
    for copy in copies:
        copy.wait_recv()

    @pl.loop(0, NZ)
    def _(t):
        for p in range(KW // 2):
            blocks = [mx[q, t, 16 * p : 16 * (p + 1)].astype(jnp.float32) for q in range(NX)]
            for q in range(2):
                rows = jnp.concatenate([b[8 * q : 8 * (q + 1)] for b in blocks], axis=0)
                k = 2 * p + q
                mbig[t, :, LANES * k : LANES * (k + 1)] = rows.astype(jnp.bfloat16)

    half_copy.wait_recv()
    vectors = jnp.concatenate([hs[0], hs[1]], axis=1)
    bias = jnp.dot(
        mbig[...].reshape(WALKERS, KW * LANES), vectors, preferred_element_type=jnp.float32
    )
    low, high = bias[:, :GROUP], bias[:, GROUP:]
    fown[...] = jnp.where(core == 0, low, high)
    fsend[...] = jnp.where(core == 0, high, low)
    spin_copy = send(fsend, frecv, mate)
    spin_copy.wait_recv()
    fz[...] = (fown[...] + frecv[...]).reshape(NZ, WALKERS // NZ, GROUP)

    fr[z] = fz[z]
    copies = []
    for d in range(1, NZ):
        t, device = at_z(d)
        copies.append(send(fz.at[t], fr.at[z], device))
    for copy in copies:
        copy.wait_recv()
    fy[...] = jnp.sum(fr[...], axis=0)
    fyr[y] = fy[...]
    copies = []
    for d in range(1, NY):
        t, device = at_y(d)
        copies.append(send(fy, fyr.at[y], device))
    load_d.wait()
    own_draw = jnp.concatenate(
        [drawbuf[pl.ds(NX * z + q, NY, stride=NX * NZ), :] for q in range(NX)], axis=0
    )
    for copy in copies:
        copy.wait_recv()
    total = jnp.sum(fyr[...], axis=0)
    sg[c, z] = (own_draw + root_step * total).astype(jnp.bfloat16)

    copies = []
    for d in range(1, NZ):
        t, device = at_z(d)
        copies.append(send(sg.at[c, z], sg.at[c, z], device))
    for copy in copies:
        copy.wait_recv()
    copies = []
    for d in range(1, NX):
        copies.append(send(sg.at[c], sg.at[c], at_x(d)[1]))
    mate_copies = [send(sg.at[c], sg.at[c], mate)]
    for d, copy in enumerate(copies, 1):
        copy.wait_recv()
        source = lax.rem(x - d + NX, NX) * 2 + core
        mate_copies.append(send(sg.at[source], sg.at[source], mate))
    for copy in mate_copies:
        copy.wait_recv()
    load_c.wait()
    for copy in chol_copies:
        copy.wait_recv()

    shifted = jnp.concatenate([sg[g].reshape(WALKERS, GROUP) for g in range(2 * NX)], axis=1)
    block = WALKERS // NZ
    for i in range(XI):
        columns = cr[:, i].reshape(2 * NX * GROUP, LH)
        product = jnp.dot(shifted, columns, preferred_element_type=jnp.float32)
        product = (root_step * product).astype(jnp.bfloat16)
        pz[:, block * i : block * (i + 1), :] = product.reshape(NZ, block, LH)

    rz[z] = pz[z]
    copies = []
    for d in range(1, NZ):
        t, device = at_z(d)
        copies.append(send(pz.at[t], rz.at[z], device))
    for copy in copies:
        copy.wait_recv()

    @pl.loop(0, NZ // 2)
    def _(pair):
        tiles = []
        for t in range(2):
            for i in range(XI):
                tiles.append(rz[2 * pair + t, block * i : block * (i + 1), :].astype(jnp.float32))
        for p in range(XI):
            for q in range(NX):
                two = [tiles[2 * p + r][8 * q : 8 * (q + 1)] for r in range(2)]
                start = pl.multiple_of(2 * XI * NY * pair + 16 * p, 16)
                qx[q, pl.ds(start, 16), :] = jnp.concatenate(two, axis=0).astype(jnp.bfloat16)

    rx[x] = qx[x]
    copies = []
    for d in range(1, NX):
        t, device = at_x(d)
        copies.append(send(qx.at[t], rx.at[x], device))
    for copy in copies:
        copy.wait_recv()

    run = XI * NY

    @pl.loop(0, NZ // 2)
    def _(pair):
        for q in range(NX):
            rows = rx[q, pl.ds(pl.multiple_of(2 * run * pair, 16), 2 * run), :].astype(jnp.float32)
            for t in range(2):
                start = pl.multiple_of((2 * NX * pair + NX * t + q) * run, 8)
                for v in range(LH // LANES):
                    gbuf[v, pl.ds(start, run), :] = rows[run * t : run * (t + 1), LANES * v : LANES * (v + 1)]

    @pl.loop(0, NY)
    def _(t):
        for v in range(LH // LANES):
            for r in range(rows_y // 16):
                two = [gbuf[v, pl.ds((16 * r + 8 * q) * NY + t, 8, stride=NY), :] for q in range(2)]
                qy[t, 16 * r : 16 * (r + 1), LANES * v : LANES * (v + 1)] = jnp.concatenate(
                    two, axis=0
                ).astype(jnp.bfloat16)

    fb[core, y] = qy[y]
    copies = []
    for d in range(1, NY):
        t, device = at_y(d)
        copies.append(send(qy.at[t], fb.at[core, y], device))
    mate_copies = [send(fb.at[core, y], fb.at[core, y], mate)]
    for d, copy in enumerate(copies, 1):
        copy.wait_recv()
        source = lax.rem(y - d + NY, NY)
        mate_copies.append(send(fb.at[core, source], fb.at[core, source], mate))
    for copy in mate_copies:
        copy.wait_recv()

    cur[...] = wt[...].astype(jnp.bfloat16)
    prop[...] = wt[...]
    for degree in range(1, 5):
        field = jnp.concatenate([fb[0].reshape(M, LH), fb[1].reshape(M, LH)], axis=1)
        term = jnp.dot(field, cur[...], preferred_element_type=jnp.float32)
        if degree > 1:
            term = term / degree
        prop[...] += term
        if degree < 4:
            cur[...] = term.astype(jnp.bfloat16)

    rows_c = M // (2 * NX)
    copies = []
    own_slot = lax.rem(w, 2) * NX + x
    for dx, dc, dp, tc, device in finals:
        start = pl.multiple_of(rows_c * tc, 8)
        copies.append(send(prop.at[pl.ds(start, rows_c)], cand.at[own_slot, core], device))
    cand[own_slot, core] = prop[pl.ds(pl.multiple_of(rows_c * c, 8), rows_c), :]

    first = lax.div(w, 2) * (2 * NX)
    sums = counts[first]
    source = [jnp.int32(0)] * NX
    for i in range(2 * NX):
        if i:
            sums = sums + counts[first + i]
        for j in range(NX):
            source[j] = source[j] + jnp.where(sums <= lax.rem(w, 2) * NX + j, 1, 0)
    source = [jnp.minimum(s, 2 * NX - 1) for s in source]
    for copy in copies:
        copy.wait_recv()
    lane = lax.broadcasted_iota(jnp.int32, (rows_c, LANES), 1)
    for j in range(NX):
        up = cand[source[j], 0]
        down = pltpu.roll(cand[source[j], 1], HALF_E - SHIFT, 1)
        out[j, :, 0:LANES] = jnp.where(lane < HALF_E, up, down)
        out[j, :, LANES : 2 * HALF_E] = down[:, : 2 * HALF_E - LANES]

    for copy in started:
        copy.wait_send()


def local(walkers, inv_intersection, half_vectors, chol_vectors, field_draw, counts):
    c = lax.axis_index("chol")
    x, core = c // 2, c % 2
    own = lax.dynamic_index_in_dim(inv_intersection, x, 0, keepdims=False)
    padded = jnp.pad(own, ((0, 0), (SHIFT, SHIFT), (SHIFT, SHIFT)))
    inverse = jnp.where(core == 0, padded[0, SHIFT:, SHIFT:], padded[1, :LANES, :LANES])
    half = half_vectors.transpose(2, 1, 0)
    chol = chol_vectors.transpose(1, 0, 2)
    f32, bf16 = jnp.float32, jnp.bfloat16
    rows_y, rows_c, block = M // NY, M // (2 * NX), WALKERS // NZ
    vmem = pltpu.VMEM
    scratch = dict(
        wbuf=vmem((2 * HALF_E, M), f32),
        wt=vmem((M, LANES), f32),
        hbuf=vmem((KW, 2 * HALF_E, GROUP), bf16),
        hs=vmem((2, KW * LANES, GROUP), bf16),
        hsend=vmem((KW * LANES, GROUP), bf16),
        m1=vmem((NY, rows_y, LANES), bf16),
        s1=vmem((NY, rows_y, LANES), bf16),
        s1f=vmem((NY * rows_y, LANES), f32),
        s2=vmem((NZ, KW * NY, LANES), bf16),
        mx=vmem((NX, NZ, KW * NY, LANES), bf16),
        mbig=vmem((NZ, block, KW * LANES), bf16),
        fsend=vmem((WALKERS, GROUP), f32),
        fown=vmem((WALKERS, GROUP), f32),
        frecv=vmem((WALKERS, GROUP), f32),
        fz=vmem((NZ, block, GROUP), f32),
        fr=vmem((NZ, block, GROUP), f32),
        fy=vmem((block, GROUP), f32),
        fyr=vmem((NY, block, GROUP), f32),
        drawbuf=vmem((WALKERS, GROUP), f32),
        sg=vmem((2 * NX, NZ, block, GROUP), bf16),
        cr=vmem((2 * NX, XI, GROUP, LH), bf16),
        pz=vmem((NZ, XI * block, LH), bf16),
        rz=vmem((NZ, XI * block, LH), bf16),
        qx=vmem((NX, NZ * XI * NY, LH), bf16),
        rx=vmem((NX, NZ * XI * NY, LH), bf16),
        gbuf=vmem((LH // LANES, NZ * NX * XI * NY, LANES), f32),
        qy=vmem((NY, rows_y, LH), bf16),
        fb=vmem((2, NY, rows_y, LH), bf16),
        cur=vmem((M, LANES), bf16),
        prop=vmem((M, LANES), f32),
        cand=vmem((2 * NX, 2, rows_c, LANES), f32),
        ssem=pltpu.SemaphoreType.DMA((COPIES,)),
        rsem=pltpu.SemaphoreType.DMA((COPIES,)),
        lsem=pltpu.SemaphoreType.DMA((4,)),
    )
    hbm = pl.BlockSpec(memory_space=pltpu.HBM)
    in_vmem = pl.BlockSpec(memory_space=pltpu.VMEM)
    in_smem = pl.BlockSpec(memory_space=pltpu.SMEM)
    result = pl.pallas_call(
        kernel,
        out_shape=jax.ShapeDtypeStruct((NX, rows_c, 2 * HALF_E), f32),
        in_specs=[hbm, in_vmem, hbm, hbm, hbm, in_smem],
        out_specs=in_vmem,
        scratch_shapes=list(scratch.values()),
        compiler_params=pltpu.CompilerParams(
            collective_id=0, has_side_effects=True, vmem_limit_bytes=48 * 2**20
        ),
    )(walkers, inverse, half, chol, field_draw, counts)
    return result.transpose(0, 2, 1)


def solution(mesh):
    placed = (
        P("walk", None, None),
        P("walk", None, None, None),
        P("chol", None, "walk"),
        P("chol", "walk", None),
        P(None, "chol"),
        P(),
    )
    return jax.shard_map(
        local, mesh=mesh, in_specs=placed, out_specs=P("walk", None, "chol"), check_vma=False
    )
```

```python
import jax
import jax.numpy as jnp
from jax import lax
from jax.experimental import pallas as pl
from jax.experimental.pallas import tpu as pltpu
from jax.sharding import PartitionSpec as P

root_step = 0.1

NX, NY, NZ = 4, 8, 8
LANES = 128
HALF_E = 100
SHIFT = LANES - HALF_E
M = 768
LH = M // 2
KW = M // (NY * NZ)
XI = KW // NX
WALKERS = NX * NY * NZ
GROUP = 128
COPIES = 256
MESH = pl.DeviceIdType.MESH


def kernel(
    walkers, inverse, half, chol, draw, counts, out,
    wbuf, wt, hbuf, hs, hsend, m1, s1, s1f, s2, mx, mbig, fz, fr, fy, fyr,
    drawbuf, sg, cr, pz, rz, qx, rx, gbuf, qy, fb, cur, prop, low, cand, ssem, rsem, lsem,
):
    c = lax.axis_index("chol")
    w = lax.axis_index("walk")
    x = lax.div(c, 2)
    core = lax.rem(c, 2)
    y = lax.div(w, NZ)
    z = lax.rem(w, NZ)
    other = 1 - core
    partner_w = w + 1 - 2 * lax.rem(w, 2)

    def at_y(d):
        t = lax.rem(y + d, NY)
        return t, (c, t * NZ + z)

    def at_z(d):
        t = lax.rem(z + d, NZ)
        return t, (c, y * NZ + t)

    def at_x(d):
        t = lax.rem(x + d, NX)
        return t, (t * 2 + core, w)

    mate = (x * 2 + other, w)

    barrier = pltpu.get_barrier_semaphore()
    greeted = 0
    peers = [at_y(d)[1] for d in range(1, NY)] + [at_z(d)[1] for d in range(1, NZ)]
    finals = []
    for dx in range(NX):
        for dc in range(2):
            tx = lax.rem(x + dx, NX)
            tc = tx * 2 + (core if dc == 0 else other)
            for dp in range(2):
                if dx or dc or dp:
                    finals.append((dx, dc, dp, tc, (tc, partner_w if dp else w)))
                    if dx or dc:
                        peers.append((tc, partner_w if dp else w))
    for peer in peers:
        pl.semaphore_signal(barrier, inc=1, device_id=peer, device_id_type=MESH)
        greeted += 1

    started = []

    def send(src, dst, device):
        i = len(started)
        copy = pltpu.make_async_remote_copy(
            src_ref=src, dst_ref=dst, send_sem=ssem.at[i], recv_sem=rsem.at[i],
            device_id=device, device_id_type=MESH,
        )
        copy.start()
        started.append(copy)
        return copy

    load_w = pltpu.make_async_copy(walkers.at[x], wbuf, lsem.at[0])
    load_h = pltpu.make_async_copy(half, hbuf, lsem.at[1])
    load_d = pltpu.make_async_copy(draw, drawbuf, lsem.at[2])
    load_c = pltpu.make_async_copy(
        chol.at[pl.ds(XI * x, XI), :, pl.ds(pl.multiple_of(LH * core, LANES), LH)], cr.at[c], lsem.at[3]
    )
    load_w.start()
    load_h.start()
    load_d.start()
    load_c.start()

    load_w.wait()
    electron = lax.broadcasted_iota(jnp.int32, (LANES, M), 0)
    up = jnp.where(electron < HALF_E, wbuf[0:LANES, :], 0.0)
    down = jnp.where(electron >= SHIFT, wbuf[2 * HALF_E - LANES : 2 * HALF_E, :], 0.0)
    wt[...] = jnp.where(core == 0, up, down).T
    mixed = lax.dot_general(
        wt[...], inverse[...], (((1,), (1,)), ((), ())),
        precision=lax.Precision.HIGHEST, preferred_element_type=jnp.float32,
    )
    m1[...] = mixed.astype(jnp.bfloat16).reshape(NY, M // NY, LANES)
    s1[y] = m1[y]

    pl.semaphore_wait(barrier, greeted)

    copies = []
    for d in range(1, NY):
        t, device = at_y(d)
        copies.append(send(m1.at[t], s1.at[y], device))

    chol_copies = []

    def send_chol(distances):
        for dx in distances:
            for dc in range(2):
                if dx or dc:
                    tx = lax.rem(x + dx, NX)
                    tcore = core if dc == 0 else other
                    columns = pl.ds(pl.multiple_of(LH * tcore, LANES), LH)
                    chol_copies.append(
                        send(chol.at[pl.ds(XI * tx, XI), :, columns], cr.at[c], (tx * 2 + tcore, w))
                    )

    send_chol((0, 1, NX - 1))

    load_h.wait()
    for k in range(KW):
        rows = hbuf[k].astype(jnp.float32)
        first = rows[0:LANES]
        second = rows[2 * HALF_E - LANES : 2 * HALF_E]
        hs[core, LANES * k : LANES * (k + 1)] = jnp.where(core == 0, first, second).astype(jnp.bfloat16)
        hsend[LANES * k : LANES * (k + 1)] = jnp.where(core == 0, second, first).astype(jnp.bfloat16)
    half_copy = send(hsend, hs.at[core], mate)

    for copy in copies:
        copy.wait_recv()

    rows_y = M // NY
    for t in range(NY):
        s1f[rows_y * t : rows_y * (t + 1)] = s1[t].astype(jnp.float32)

    @pl.loop(0, NZ)
    def _(t):
        for p in range(KW // 2):
            pair = [s1f[pl.ds(KW * t + 2 * p + q, NY, stride=rows_y), :] for q in range(2)]
            s2[t, 16 * p : 16 * (p + 1)] = jnp.concatenate(pair, axis=0).astype(jnp.bfloat16)

    mx[x, z] = s2[z]
    copies = []
    for d in range(1, NZ):
        t, device = at_z(d)
        copies.append(send(s2.at[t], mx.at[x, z], device))

    x_copies = []
    for d in range(NZ):
        if d:
            copies[d - 1].wait_recv()
        source = lax.rem(z - d + NZ, NZ)
        for e in range(1, NX):
            x_copies.append(send(mx.at[x, source], mx.at[x, source], at_x(e)[1]))
    for copy in x_copies:
        copy.wait_recv()
    send_chol(range(2, NX - 1))

    @pl.loop(0, NZ)
    def _(t):
        for p in range(KW // 2):
            blocks = [mx[q, t, 16 * p : 16 * (p + 1)].astype(jnp.float32) for q in range(NX)]
            for q in range(2):
                rows = jnp.concatenate([b[8 * q : 8 * (q + 1)] for b in blocks], axis=0)
                k = 2 * p + q
                mbig[t, :, LANES * k : LANES * (k + 1)] = rows.astype(jnp.bfloat16)

    half_copy.wait_recv()
    vectors = jnp.concatenate([hs[0], hs[1]], axis=1)
    bias = jnp.dot(
        mbig[...].reshape(WALKERS, KW * LANES), vectors, preferred_element_type=jnp.float32
    )
    for q in range(2):
        part = bias[:, GROUP * q : GROUP * (q + 1)].astype(jnp.bfloat16)
        fz[q] = part.reshape(NZ, WALKERS // NZ, GROUP)

    fr[core, z] = fz[core, z]
    copies = []
    for d in range(NZ):
        t, _ = at_z(d)
        for tcore in (core, other) if d else (other,):
            copies.append(send(fz.at[tcore, t], fr.at[core, z], (x * 2 + tcore, y * NZ + t)))
    for copy in copies:
        copy.wait_recv()
    fy[...] = jnp.sum(fr[...].astype(jnp.float32), axis=(0, 1)).astype(jnp.bfloat16)
    fyr[y] = fy[...]
    copies = []
    for d in range(1, NY):
        t, device = at_y(d)
        copies.append(send(fy, fyr.at[y], device))
    load_d.wait()
    own_draw = jnp.concatenate(
        [drawbuf[pl.ds(NX * z + q, NY, stride=NX * NZ), :] for q in range(NX)], axis=0
    )
    for copy in copies:
        copy.wait_recv()
    total = jnp.sum(fyr[...].astype(jnp.float32), axis=0)
    sg[c, z] = (own_draw + root_step * total).astype(jnp.bfloat16)

    copies = []
    for d in range(1, NZ):
        t, device = at_z(d)
        copies.append(send(sg.at[c, z], sg.at[c, z], device))
    for copy in copies:
        copy.wait_recv()
    copies = []
    for d in range(1, NX):
        copies.append(send(sg.at[c], sg.at[c], at_x(d)[1]))
    mate_copies = [send(sg.at[c], sg.at[c], mate)]
    for d, copy in enumerate(copies, 1):
        copy.wait_recv()
        source = lax.rem(x - d + NX, NX) * 2 + core
        mate_copies.append(send(sg.at[source], sg.at[source], mate))
    for copy in mate_copies:
        copy.wait_recv()
    load_c.wait()
    for copy in chol_copies:
        copy.wait_recv()

    shifted = jnp.concatenate([sg[g].reshape(WALKERS, GROUP) for g in range(2 * NX)], axis=1)
    block = WALKERS // NZ
    run = XI * NY

    def to_z(v):
        for i in range(XI):
            columns = cr[:, i, :, LANES * v : LANES * (v + 1)].reshape(2 * NX * GROUP, LANES)
            product = jnp.dot(shifted, columns, preferred_element_type=jnp.float32)
            product = (root_step * product).astype(jnp.bfloat16)
            pz[v, :, block * i : block * (i + 1), :] = product.reshape(NZ, block, LANES)
        rz[v, z] = pz[v, z]
        copies = []
        for d in range(1, NZ):
            t, device = at_z(d)
            copies.append(send(pz.at[v, t], rz.at[v, z], device))
        return copies

    def to_x(v):
        @pl.loop(0, NZ // 2)
        def _(pair):
            tiles = []
            for t in range(2):
                for i in range(XI):
                    tiles.append(rz[v, 2 * pair + t, block * i : block * (i + 1), :].astype(jnp.float32))
            for p in range(XI):
                for q in range(NX):
                    two = [tiles[2 * p + r][8 * q : 8 * (q + 1)] for r in range(2)]
                    start = pl.multiple_of(2 * run * pair + 16 * p, 16)
                    qx[v, q, pl.ds(start, 16), :] = jnp.concatenate(two, axis=0).astype(jnp.bfloat16)

        rx[v, x] = qx[v, x]
        copies = []
        for d in range(1, NX):
            t, device = at_x(d)
            copies.append(send(qx.at[v, t], rx.at[v, x], device))
        return copies

    def to_y(v):
        @pl.loop(0, NZ // 2)
        def _(pair):
            for q in range(NX):
                rows = rx[v, q, pl.ds(pl.multiple_of(2 * run * pair, 16), 2 * run), :].astype(jnp.float32)
                for t in range(2):
                    start = pl.multiple_of((2 * NX * pair + NX * t + q) * run, 8)
                    gbuf[v, pl.ds(start, run), :] = rows[run * t : run * (t + 1)]

        @pl.loop(0, NY)
        def _(t):
            for r in range(rows_y // 16):
                two = [gbuf[v, pl.ds((16 * r + 8 * q) * NY + t, 8, stride=NY), :] for q in range(2)]
                qy[v, t, 16 * r : 16 * (r + 1), :] = jnp.concatenate(two, axis=0).astype(jnp.bfloat16)

        fb[core, v, y] = qy[v, y]
        copies = []
        for d in range(1, NY):
            t, device = at_y(d)
            copies.append(send(qy.at[v, t], fb.at[core, v, y], device))
        return copies

    def to_mate(v, copies):
        mates = []
        for d in range(NY):
            if d:
                copies[d - 1].wait_recv()
            source = lax.rem(y - d + NY, NY)
            mates.append(send(fb.at[core, v, source], fb.at[core, v, source], mate))
        return mates

    chunks = LH // LANES
    in_z = [to_z(v) for v in range(chunks)]
    in_x, in_y, in_mate = [], [], []
    for step in range(chunks + 2):
        if step < chunks:
            for copy in in_z[step]:
                copy.wait_recv()
            in_x.append(to_x(step))
        if 0 <= step - 1 < chunks:
            for copy in in_x[step - 1]:
                copy.wait_recv()
            in_y.append(to_y(step - 1))
        if 0 <= step - 2 < chunks:
            in_mate += to_mate(step - 2, in_y[step - 2])
    for copy in in_mate:
        copy.wait_recv()

    cur[...] = wt[...].astype(jnp.bfloat16)
    prop[...] = wt[...]
    for degree in range(1, 5):
        field = jnp.concatenate(
            [fb[q, v].reshape(M, LANES) for q in range(2) for v in range(chunks)], axis=1
        )
        term = jnp.dot(field, cur[...], preferred_element_type=jnp.float32)
        if degree > 1:
            term = term / degree
        prop[...] += term
        if degree < 4:
            cur[...] = term.astype(jnp.bfloat16)

    rows_c = M // (2 * NX)
    low[...] = prop[...].astype(jnp.bfloat16)
    copies = []
    own_slot = lax.rem(w, 2) * NX + x
    for dx, dc, dp, tc, device in finals:
        start = pl.multiple_of(rows_c * tc, 16)
        copies.append(send(low.at[pl.ds(start, rows_c)], cand.at[own_slot, core], device))
    cand[own_slot, core] = low[pl.ds(pl.multiple_of(rows_c * c, 16), rows_c), :]

    first = lax.div(w, 2) * (2 * NX)
    sums = counts[first]
    source = [jnp.int32(0)] * NX
    for i in range(2 * NX):
        if i:
            sums = sums + counts[first + i]
        for j in range(NX):
            source[j] = source[j] + jnp.where(sums <= lax.rem(w, 2) * NX + j, 1, 0)
    source = [jnp.minimum(s, 2 * NX - 1) for s in source]
    for copy in copies:
        copy.wait_recv()
    lane = lax.broadcasted_iota(jnp.int32, (rows_c, LANES), 1)
    for j in range(NX):
        up = cand[source[j], 0].astype(jnp.float32)
        down = pltpu.roll(cand[source[j], 1].astype(jnp.float32), HALF_E - SHIFT, 1)
        out[j, :, 0:LANES] = jnp.where(lane < HALF_E, up, down)
        out[j, :, LANES : 2 * HALF_E] = down[:, : 2 * HALF_E - LANES]

    for copy in started:
        copy.wait_send()


def local(walkers, inv_intersection, half_vectors, chol_vectors, field_draw, counts):
    c = lax.axis_index("chol")
    x, core = c // 2, c % 2
    own = lax.dynamic_index_in_dim(inv_intersection, x, 0, keepdims=False)
    padded = jnp.pad(own, ((0, 0), (SHIFT, SHIFT), (SHIFT, SHIFT)))
    inverse = jnp.where(core == 0, padded[0, SHIFT:, SHIFT:], padded[1, :LANES, :LANES])
    half = half_vectors.transpose(2, 1, 0)
    chol = chol_vectors.transpose(1, 0, 2)
    f32, bf16 = jnp.float32, jnp.bfloat16
    rows_y, rows_c, block = M // NY, M // (2 * NX), WALKERS // NZ
    chunks = LH // LANES
    vmem = pltpu.VMEM
    scratch = dict(
        wbuf=vmem((2 * HALF_E, M), f32),
        wt=vmem((M, LANES), f32),
        hbuf=vmem((KW, 2 * HALF_E, GROUP), bf16),
        hs=vmem((2, KW * LANES, GROUP), bf16),
        hsend=vmem((KW * LANES, GROUP), bf16),
        m1=vmem((NY, rows_y, LANES), bf16),
        s1=vmem((NY, rows_y, LANES), bf16),
        s1f=vmem((NY * rows_y, LANES), f32),
        s2=vmem((NZ, KW * NY, LANES), bf16),
        mx=vmem((NX, NZ, KW * NY, LANES), bf16),
        mbig=vmem((NZ, block, KW * LANES), bf16),
        fz=vmem((2, NZ, block, GROUP), bf16),
        fr=vmem((2, NZ, block, GROUP), bf16),
        fy=vmem((block, GROUP), bf16),
        fyr=vmem((NY, block, GROUP), bf16),
        drawbuf=vmem((WALKERS, GROUP), f32),
        sg=vmem((2 * NX, NZ, block, GROUP), bf16),
        cr=vmem((2 * NX, XI, GROUP, LH), bf16),
        pz=vmem((chunks, NZ, XI * block, LANES), bf16),
        rz=vmem((chunks, NZ, XI * block, LANES), bf16),
        qx=vmem((chunks, NX, NZ * XI * NY, LANES), bf16),
        rx=vmem((chunks, NX, NZ * XI * NY, LANES), bf16),
        gbuf=vmem((chunks, NZ * NX * XI * NY, LANES), f32),
        qy=vmem((chunks, NY, rows_y, LANES), bf16),
        fb=vmem((2, chunks, NY, rows_y, LANES), bf16),
        cur=vmem((M, LANES), bf16),
        prop=vmem((M, LANES), f32),
        low=vmem((M, LANES), bf16),
        cand=vmem((2 * NX, 2, rows_c, LANES), bf16),
        ssem=pltpu.SemaphoreType.DMA((COPIES,)),
        rsem=pltpu.SemaphoreType.DMA((COPIES,)),
        lsem=pltpu.SemaphoreType.DMA((4,)),
    )
    hbm = pl.BlockSpec(memory_space=pltpu.HBM)
    in_vmem = pl.BlockSpec(memory_space=pltpu.VMEM)
    in_smem = pl.BlockSpec(memory_space=pltpu.SMEM)
    result = pl.pallas_call(
        kernel,
        out_shape=jax.ShapeDtypeStruct((NX, rows_c, 2 * HALF_E), f32),
        in_specs=[hbm, in_vmem, hbm, hbm, hbm, in_smem],
        out_specs=in_vmem,
        scratch_shapes=list(scratch.values()),
        compiler_params=pltpu.CompilerParams(
            collective_id=0, has_side_effects=True, vmem_limit_bytes=63 * 2**20
        ),
    )(walkers, inverse, half, chol, field_draw, counts)
    return result.transpose(0, 2, 1)


def solution(mesh):
    placed = (
        P("walk", None, None),
        P("walk", None, None, None),
        P("chol", None, "walk"),
        P("chol", "walk", None),
        P(None, "chol"),
        P(),
    )
    return jax.shard_map(
        local, mesh=mesh, in_specs=placed, out_specs=P("walk", None, "chol"), check_vma=False
    )
```

```python
import jax
import jax.numpy as jnp
from jax import lax
from jax.experimental import pallas as pl
from jax.experimental.pallas import tpu as pltpu
from jax.sharding import PartitionSpec as P

root_step = 0.1

NX, NY, NZ = 4, 8, 8
LANES = 128
HALF_E = 100
SHIFT = LANES - HALF_E
M = 768
LH = M // 2
KW = M // (NY * NZ)
XI = KW // NX
WALKERS = NX * NY * NZ
GROUP = 128
COPIES = 256
FAR_FIRST = (4, 3, 5, 2, 6, 1, 7)
NEAR_FIRST = (1, 7, 2, 6, 3, 5, 4)
CHOL_FIRST = ((1, 0), (3, 0), (0, 1), (1, 1), (3, 1))
CHOL_LAST = ((2, 0), (2, 1))
MESH = pl.DeviceIdType.MESH


def kernel(
    walkers, inverse, half, chol, draw, counts, out,
    wbuf, ibuf, ipad, wt, hbuf, hs, hsend, m1, s1, s1f, s2, mx, mbig, swap, psend, precv, fz, fr, fy, fyr,
    drawbuf, owndraw, sg, cr, pz, rz, qx, rx, gbuf, qy, rb, fb, cur, prop, low, cand, ssem, rsem, lsem,
):
    c = lax.axis_index("chol")
    w = lax.axis_index("walk")
    x = lax.div(c, 2)
    core = lax.rem(c, 2)
    y = lax.div(w, NZ)
    z = lax.rem(w, NZ)
    other = 1 - core
    partner_w = w + 1 - 2 * lax.rem(w, 2)

    p = z + core * (y - z)
    q = y + core * (z - y)
    step_p, step_q = 1 + (NZ - 1) * core, NZ - (NZ - 1) * core

    def at_p(d):
        t = lax.rem(p + d, NZ)
        return t, (c, t * step_p + q * step_q)

    def at_q(d):
        t = lax.rem(q + d, NY)
        return t, (c, p * step_p + t * step_q)

    def at_x(d):
        t = lax.rem(x + d, NX)
        return t, (t * 2 + core, w)

    mate = (x * 2 + other, w)

    barrier = pltpu.get_barrier_semaphore()
    greeted = 0
    peers = [at_q(d)[1] for d in range(1, NY)] + [at_p(d)[1] for d in range(1, NZ)]
    finals = []
    for dx in range(NX):
        for dc in range(2):
            tx = lax.rem(x + dx, NX)
            tc = tx * 2 + (core if dc == 0 else other)
            for dp in range(2):
                if dx or dc or dp:
                    finals.append((dx, dc, dp, tc, (tc, partner_w if dp else w)))
                    if dx or dc:
                        peers.append((tc, partner_w if dp else w))
    for peer in peers:
        pl.semaphore_signal(barrier, inc=1, device_id=peer, device_id_type=MESH)
        greeted += 1

    started = []

    def send(src, dst, device):
        i = len(started)
        copy = pltpu.make_async_remote_copy(
            src_ref=src, dst_ref=dst, send_sem=ssem.at[i], recv_sem=rsem.at[i],
            device_id=device, device_id_type=MESH,
        )
        copy.start()
        started.append(copy)
        return copy

    load_w = pltpu.make_async_copy(walkers.at[x], wbuf, lsem.at[0])
    load_h = pltpu.make_async_copy(half, hbuf, lsem.at[1])
    load_d = pltpu.make_async_copy(draw, drawbuf, lsem.at[2])
    load_c = pltpu.make_async_copy(
        chol.at[pl.ds(XI * x, XI), :, pl.ds(pl.multiple_of(LH * core, LANES), LH)], cr.at[c], lsem.at[3]
    )
    load_i = pltpu.make_async_copy(inverse.at[x], ibuf, lsem.at[4])
    load_i.start()
    load_w.start()
    load_h.start()
    load_d.start()
    load_c.start()

    load_w.wait()
    electron = lax.broadcasted_iota(jnp.int32, (LANES, M), 0)
    up = jnp.where(electron < HALF_E, wbuf[0:LANES, :], 0.0)
    down = jnp.where(electron >= SHIFT, wbuf[2 * HALF_E - LANES : 2 * HALF_E, :], 0.0)
    wt[...] = jnp.where(core == 0, up, down).T
    wide = wt[...]
    wide_hi = wide.astype(jnp.bfloat16)
    wide_lo = (wide - wide_hi.astype(jnp.float32)).astype(jnp.bfloat16)
    load_i.wait()
    ipad[...] = jnp.zeros_like(ipad)
    ipad[0:HALF_E, 0:HALF_E] = ibuf[pl.ds(core, HALF_E, stride=2), :]
    inv = ipad[...]
    inv = jnp.where(core == 0, inv, pltpu.roll(pltpu.roll(inv, SHIFT, 0), SHIFT, 1))
    inv_hi = inv.astype(jnp.bfloat16)
    inv_lo = (inv - inv_hi.astype(jnp.float32)).astype(jnp.bfloat16)
    mixed = lax.dot_general(
        jnp.concatenate([wide_hi, wide_lo, wide_hi, wide_lo], axis=1),
        jnp.concatenate([inv_hi, inv_hi, inv_lo, inv_lo], axis=1),
        (((1,), (1,)), ((), ())),
        preferred_element_type=jnp.float32,
    )
    rows_y = M // NY

    @pl.when(core == 0)
    def _():
        m1[...] = mixed.astype(jnp.bfloat16).reshape(NY, rows_y, LANES)

    @pl.when(core == 1)
    def _():
        s1f[...] = mixed

        @pl.loop(0, NZ)
        def _(t):
            for r in range(KW // 2):
                pair = [s1f[pl.ds(KW * t + 2 * r + h, NY, stride=rows_y), :] for h in range(2)]
                m1[t, 16 * r : 16 * (r + 1)] = jnp.concatenate(pair, axis=0).astype(jnp.bfloat16)

    s1[q] = m1[q]

    pl.semaphore_wait(barrier, greeted)

    copies = []
    for d in FAR_FIRST:
        t, device = at_q(d)
        copies.append(send(m1.at[t], s1.at[q], device))

    chol_copies = []

    def send_chol(pieces):
        for dx, dc in pieces:
            tx = lax.rem(x + dx, NX)
            tcore = core if dc == 0 else other
            columns = pl.ds(pl.multiple_of(LH * tcore, LANES), LH)
            chol_copies.append(
                send(chol.at[pl.ds(XI * tx, XI), :, columns], cr.at[c], (tx * 2 + tcore, w))
            )

    send_chol(CHOL_FIRST)

    load_h.wait()
    for k in range(KW):
        rows = hbuf[k].astype(jnp.float32)
        first = rows[0:LANES]
        second = rows[2 * HALF_E - LANES : 2 * HALF_E]
        hs[core, LANES * k : LANES * (k + 1)] = jnp.where(core == 0, first, second).astype(jnp.bfloat16)
        hsend[LANES * k : LANES * (k + 1)] = jnp.where(core == 0, second, first).astype(jnp.bfloat16)
    half_copy = send(hsend, hs.at[core], mate)

    row = lax.broadcasted_iota(jnp.int32, (WALKERS, WALKERS), 0)
    column = lax.broadcasted_iota(jnp.int32, (WALKERS, WALKERS), 1)
    target = (row & 7) * (WALKERS // NZ) + (row & 24) + (row >> 5)
    swap[...] = jnp.where(column == target, 1.0, 0.0).astype(jnp.bfloat16)

    load_d.wait()

    @pl.when(core == 0)
    def _():
        for g in range(NX):
            owndraw[8 * g : 8 * (g + 1)] = drawbuf[pl.ds(NX * z + g, NY, stride=NX * NZ), :]

    @pl.when(core == 1)
    def _():
        for g in range(NX):
            owndraw[8 * g : 8 * (g + 1)] = drawbuf[pl.ds(NX * NZ * y + g, NZ, stride=NX), :]

    for copy in copies:
        copy.wait_recv()

    for t in range(NY):
        s1f[rows_y * t : rows_y * (t + 1)] = s1[t].astype(jnp.float32)

    @pl.loop(0, NZ)
    def _(t):
        for r in range(KW // 2):
            pair = []
            for h in range(2):
                first = t * (KW - (KW - 1) * core) + (2 * r + h) * (1 + (NY - 1) * core)
                pair.append(s1f[pl.ds(first, NY, stride=rows_y), :])
            s2[t, 16 * r : 16 * (r + 1)] = jnp.concatenate(pair, axis=0).astype(jnp.bfloat16)

    mx[x, p] = s2[p]
    copies = []
    for d in FAR_FIRST:
        t, device = at_p(d)
        copies.append(send(s2.at[t], mx.at[x, p], device))

    x_copies = []
    for d in (0,) + NEAR_FIRST:
        if d:
            copies[FAR_FIRST.index(d)].wait_recv()
        source = lax.rem(p - d + NZ, NZ)
        for e in (2, 1, 3):
            x_copies.append(send(mx.at[x, source], mx.at[x, source], at_x(e)[1]))
    for copy in x_copies:
        copy.wait_recv()
    send_chol(CHOL_LAST)

    @pl.loop(0, NZ)
    def _(t):
        for r in range(KW // 2):
            blocks = [mx[g, t, 16 * r : 16 * (r + 1)].astype(jnp.float32) for g in range(NX)]
            for h in range(2):
                rows = jnp.concatenate([b[8 * h : 8 * (h + 1)] for b in blocks], axis=0)
                k = 2 * r + h
                mbig[t, :, LANES * k : LANES * (k + 1)] = rows.astype(jnp.bfloat16)

    half_copy.wait_recv()
    vectors = jnp.concatenate([hs[0], hs[1]], axis=1)
    bias = jnp.dot(
        mbig[...].reshape(WALKERS, KW * LANES), vectors, preferred_element_type=jnp.float32
    )
    low_part, high_part = bias[:, :GROUP], bias[:, GROUP:]
    theirs = jnp.where(core == 0, high_part, low_part).astype(jnp.bfloat16)
    psend[...] = jnp.dot(swap[...], theirs, preferred_element_type=jnp.float32).astype(jnp.bfloat16)
    spin_copy = send(psend, precv, mate)
    ours = jnp.where(core == 0, low_part, high_part)
    spin_copy.wait_recv()
    both = (ours + precv[...].astype(jnp.float32)).astype(jnp.bfloat16)
    fz[...] = both.reshape(NZ, WALKERS // NZ, GROUP)

    fr[p] = fz[p]
    copies = []
    for d in FAR_FIRST:
        t, device = at_p(d)
        copies.append(send(fz.at[t], fr.at[p], device))
    for copy in copies:
        copy.wait_recv()
    fy[...] = jnp.sum(fr[...].astype(jnp.float32), axis=0).astype(jnp.bfloat16)
    fyr[q] = fy[...]
    copies = []
    for d in FAR_FIRST:
        t, device = at_q(d)
        copies.append(send(fy, fyr.at[q], device))
    for copy in copies:
        copy.wait_recv()
    total = jnp.sum(fyr[...].astype(jnp.float32), axis=0)
    sg[c, p] = (owndraw[...] + root_step * total).astype(jnp.bfloat16)

    copies = []
    for d in FAR_FIRST:
        t, device = at_p(d)
        copies.append(send(sg.at[c, p], sg.at[c, p], device))
    x_copies = []
    for d in (0,) + NEAR_FIRST:
        if d:
            copies[FAR_FIRST.index(d)].wait_recv()
        source = lax.rem(p - d + NZ, NZ)
        for e in (2, 1, 3):
            x_copies.append((e, send(sg.at[c, source], sg.at[c, source], at_x(e)[1])))
    mate_copies = [send(sg.at[c], sg.at[c], mate)]
    for e in (1, 3, 2):
        for offset, copy in x_copies:
            if offset == e:
                copy.wait_recv()
        source = lax.rem(x - e + NX, NX) * 2 + core
        mate_copies.append(send(sg.at[source], sg.at[source], mate))
    for copy in mate_copies:
        copy.wait_recv()
    load_c.wait()
    for copy in chol_copies:
        copy.wait_recv()

    shifted = jnp.concatenate([sg[2 * g + core].reshape(WALKERS, GROUP) for g in range(NX)], axis=1)
    swapped = jnp.concatenate([sg[2 * g + other].reshape(WALKERS, GROUP) for g in range(NX)], axis=1)
    swapped = jnp.dot(swap[...], swapped, preferred_element_type=jnp.float32).astype(jnp.bfloat16)
    shifted = jnp.concatenate([shifted, swapped], axis=1)
    block = WALKERS // NZ
    run = XI * NY

    def to_p(v):
        lanes = slice(LANES * v, LANES * (v + 1))
        columns = jnp.concatenate(
            [
                jnp.concatenate([cr[2 * g + h, i, :, lanes] for i in range(XI)], axis=1)
                for h in (core, other)
                for g in range(NX)
            ],
            axis=0,
        )
        product = jnp.dot(shifted, columns, preferred_element_type=jnp.float32)
        product = (root_step * product).astype(jnp.bfloat16)
        for i in range(XI):
            part = product[:, LANES * i : LANES * (i + 1)]
            pz[v, :, block * i : block * (i + 1), :] = part.reshape(NZ, block, LANES)
        rz[v, p] = pz[v, p]
        copies = []
        for d in FAR_FIRST:
            t, device = at_p(d)
            copies.append(send(pz.at[v, t], rz.at[v, p], device))
        return copies

    def to_x(v):
        @pl.loop(0, NZ // 2)
        def _(pair):
            tiles = []
            for t in range(2):
                for i in range(XI):
                    tiles.append(rz[v, 2 * pair + t, block * i : block * (i + 1), :].astype(jnp.float32))
            for r in range(XI):
                for g in range(NX):
                    two = [tiles[2 * r + h][8 * g : 8 * (g + 1)] for h in range(2)]
                    start = pl.multiple_of(2 * run * pair + 16 * r, 16)
                    qx[v, g, pl.ds(start, 16), :] = jnp.concatenate(two, axis=0).astype(jnp.bfloat16)

        rx[v, x] = qx[v, x]
        copies = []
        for d in range(1, NX):
            t, device = at_x(d)
            copies.append(send(qx.at[v, t], rx.at[v, x], device))
        return copies

    def strided(v, put):
        @pl.loop(0, NY)
        def _(t):
            for r in range(rows_y // 16):
                two = [gbuf[v, pl.ds((16 * r + 8 * h) * NY + t, 8, stride=NY), :] for h in range(2)]
                put(t, 16 * r, jnp.concatenate(two, axis=0).astype(jnp.bfloat16))

    def to_q(v):
        @pl.loop(0, NZ // 2)
        def _(pair):
            for g in range(NX):
                rows = rx[v, g, pl.ds(pl.multiple_of(2 * run * pair, 16), 2 * run), :].astype(jnp.float32)
                for t in range(2):
                    for i in range(XI):
                        at = (2 * pair + t) * (KW - (KW - 1) * core) + (XI * g + i) * (1 + (NY - 1) * core)
                        start = pl.multiple_of(NY * at, 8)
                        gbuf[v, pl.ds(start, 8), :] = rows[run * t + 8 * i : run * t + 8 * (i + 1)]

        def put(t, r, rows):
            qy[v, t, r : r + 16, :] = rows

        strided(v, put)
        rb[v, q] = qy[v, q]
        copies = []
        for d in FAR_FIRST:
            t, device = at_q(d)
            copies.append(send(qy.at[v, t], rb.at[v, q], device))
        return copies

    def to_mate(v):
        @pl.when(core == 0)
        def _():
            fb[0, v] = rb[v]

        @pl.when(core == 1)
        def _():
            gbuf[v] = rb[v].astype(jnp.float32).reshape(M, LANES)

            def put(t, r, rows):
                fb[1, v, t, r : r + 16, :] = rows

            strided(v, put)

        return send(fb.at[core, v], fb.at[core, v], mate)

    chunks = LH // LANES
    in_p = [to_p(v) for v in range(chunks)]
    in_x, in_q, in_mate = [], [], []
    for step in range(chunks + 2):
        if step < chunks:
            for copy in in_p[step]:
                copy.wait_recv()
            in_x.append(to_x(step))
        if 0 <= step - 1 < chunks:
            for copy in in_x[step - 1]:
                copy.wait_recv()
            in_q.append(to_q(step - 1))
        if 0 <= step - 2 < chunks:
            for copy in in_q[step - 2]:
                copy.wait_recv()
            in_mate.append(to_mate(step - 2))
    for copy in in_mate:
        copy.wait_recv()

    cur[...] = wt[...].astype(jnp.bfloat16)
    prop[...] = wt[...]
    for degree in range(1, 5):
        field = jnp.concatenate(
            [fb[q, v].reshape(M, LANES) for q in range(2) for v in range(chunks)], axis=1
        )
        term = jnp.dot(field, cur[...], preferred_element_type=jnp.float32)
        if degree > 1:
            term = term / degree
        prop[...] += term
        if degree < 4:
            cur[...] = term.astype(jnp.bfloat16)

    rows_c = M // (2 * NX)
    low[...] = prop[...].astype(jnp.bfloat16)
    copies = []
    own_slot = lax.rem(w, 2) * NX + x
    for dx, dc, dp, tc, device in finals:
        start = pl.multiple_of(rows_c * tc, 16)
        copies.append(send(low.at[pl.ds(start, rows_c)], cand.at[own_slot, core], device))
    cand[own_slot, core] = low[pl.ds(pl.multiple_of(rows_c * c, 16), rows_c), :]

    first = lax.div(w, 2) * (2 * NX)
    sums = counts[first]
    source = [jnp.int32(0)] * NX
    for i in range(2 * NX):
        if i:
            sums = sums + counts[first + i]
        for j in range(NX):
            source[j] = source[j] + jnp.where(sums <= lax.rem(w, 2) * NX + j, 1, 0)
    source = [jnp.minimum(s, 2 * NX - 1) for s in source]
    for copy in copies:
        copy.wait_recv()
    lane = lax.broadcasted_iota(jnp.int32, (rows_c, LANES), 1)
    for j in range(NX):
        up = cand[source[j], 0].astype(jnp.float32)
        down = pltpu.roll(cand[source[j], 1].astype(jnp.float32), HALF_E - SHIFT, 1)
        out[j, :, 0:LANES] = jnp.where(lane < HALF_E, up, down)
        out[j, :, LANES : 2 * HALF_E] = down[:, : 2 * HALF_E - LANES]

    for copy in started:
        copy.wait_send()


def local(walkers, inv_intersection, half_vectors, chol_vectors, field_draw, counts):
    inverse = inv_intersection.transpose(0, 2, 1, 3).reshape(NX, 2 * HALF_E, HALF_E)
    half = half_vectors.transpose(2, 1, 0)
    chol = chol_vectors.transpose(1, 0, 2)
    f32, bf16 = jnp.float32, jnp.bfloat16
    rows_y, rows_c, block = M // NY, M // (2 * NX), WALKERS // NZ
    chunks = LH // LANES
    vmem = pltpu.VMEM
    scratch = dict(
        wbuf=vmem((2 * HALF_E, M), f32),
        ibuf=vmem((2 * HALF_E, HALF_E), f32),
        ipad=vmem((LANES, LANES), f32),
        wt=vmem((M, LANES), f32),
        hbuf=vmem((KW, 2 * HALF_E, GROUP), bf16),
        hs=vmem((2, KW * LANES, GROUP), bf16),
        hsend=vmem((KW * LANES, GROUP), bf16),
        m1=vmem((NY, rows_y, LANES), bf16),
        s1=vmem((NY, rows_y, LANES), bf16),
        s1f=vmem((NY * rows_y, LANES), f32),
        s2=vmem((NZ, KW * NY, LANES), bf16),
        mx=vmem((NX, NZ, KW * NY, LANES), bf16),
        mbig=vmem((NZ, block, KW * LANES), bf16),
        swap=vmem((WALKERS, WALKERS), bf16),
        psend=vmem((WALKERS, GROUP), bf16),
        precv=vmem((WALKERS, GROUP), bf16),
        fz=vmem((NZ, block, GROUP), bf16),
        fr=vmem((NZ, block, GROUP), bf16),
        fy=vmem((block, GROUP), bf16),
        fyr=vmem((NY, block, GROUP), bf16),
        drawbuf=vmem((WALKERS, GROUP), f32),
        owndraw=vmem((block, GROUP), f32),
        sg=vmem((2 * NX, NZ, block, GROUP), bf16),
        cr=vmem((2 * NX, XI, GROUP, LH), bf16),
        pz=vmem((chunks, NZ, XI * block, LANES), bf16),
        rz=vmem((chunks, NZ, XI * block, LANES), bf16),
        qx=vmem((chunks, NX, NZ * XI * NY, LANES), bf16),
        rx=vmem((chunks, NX, NZ * XI * NY, LANES), bf16),
        gbuf=vmem((chunks, NZ * NX * XI * NY, LANES), f32),
        qy=vmem((chunks, NY, rows_y, LANES), bf16),
        rb=vmem((chunks, NY, rows_y, LANES), bf16),
        fb=vmem((2, chunks, NY, rows_y, LANES), bf16),
        cur=vmem((M, LANES), bf16),
        prop=vmem((M, LANES), f32),
        low=vmem((M, LANES), bf16),
        cand=vmem((2 * NX, 2, rows_c, LANES), bf16),
        ssem=pltpu.SemaphoreType.DMA((COPIES,)),
        rsem=pltpu.SemaphoreType.DMA((COPIES,)),
        lsem=pltpu.SemaphoreType.DMA((5,)),
    )
    hbm = pl.BlockSpec(memory_space=pltpu.HBM)
    in_vmem = pl.BlockSpec(memory_space=pltpu.VMEM)
    in_smem = pl.BlockSpec(memory_space=pltpu.SMEM)
    result = pl.pallas_call(
        kernel,
        out_shape=jax.ShapeDtypeStruct((NX, rows_c, 2 * HALF_E), f32),
        in_specs=[hbm, hbm, hbm, hbm, hbm, in_smem],
        out_specs=in_vmem,
        scratch_shapes=list(scratch.values()),
        compiler_params=pltpu.CompilerParams(
            collective_id=0, has_side_effects=True, vmem_limit_bytes=63 * 2**20
        ),
    )(walkers, inverse, half, chol, field_draw, counts)
    return result.transpose(0, 2, 1)


def solution(mesh):
    placed = (
        P("walk", None, None),
        P("walk", None, None, None),
        P("chol", None, "walk"),
        P("chol", "walk", None),
        P(None, "chol"),
        P(),
    )
    return jax.shard_map(
        local, mesh=mesh, in_specs=placed, out_specs=P("walk", None, "chol"), check_vma=False
    )
```

```python
import jax
import jax.numpy as jnp
from jax import lax
from jax.experimental import pallas as pl
from jax.experimental.pallas import tpu as pltpu
from jax.sharding import PartitionSpec as P

root_step = 0.1

NX, NY, NZ = 4, 8, 8
LANES = 128
HALF_E = 100
SHIFT = LANES - HALF_E
M = 768
LH = M // 2
KW = M // (NY * NZ)
XI = KW // NX
WALKERS = NX * NY * NZ
GROUP = 128
COPIES = 256
FAR_FIRST = (4, 3, 5, 2, 6, 1, 7)
NEAR_FIRST = (1, 7, 2, 6, 3, 5, 4)
NEAR = ((1, 0), (3, 0), (1, 1), (3, 1))
FAR = ((2, 0), (2, 1))
MATE = tuple((0, 1, v) for v in range(3))
NEARS = [tuple((dx, dc, v) for dx, dc in NEAR) for v in range(3)]
FARS = [tuple((dx, dc, v) for dx, dc in FAR) for v in range(3)]
CHOL_PLAN = (MATE + NEARS[0] + NEARS[1], FARS[0] + FARS[1], NEARS[2], FARS[2], ())
BIAS_PARTS = 2
MESH = pl.DeviceIdType.MESH


def kernel(
    walkers, inverse, half, chol, draw, counts, out,
    wbuf, ibuf, ipad, wt, hbuf, hs, hsend, m1, s1, s1f, s2, mx, mbig, biasbuf, swap, psend, precv, fz, fr, fy, fyr,
    drawbuf, owndraw, sg, cbuf, cr, pz, rz, qx, rx, gbuf, qy, rb, fb, cur, prop, low, cand, ssem, rsem, lsem,
):
    c = lax.axis_index("chol")
    w = lax.axis_index("walk")
    x = lax.div(c, 2)
    core = lax.rem(c, 2)
    y = lax.div(w, NZ)
    z = lax.rem(w, NZ)
    other = 1 - core
    partner_w = w + 1 - 2 * lax.rem(w, 2)

    p = z + core * (y - z)
    q = y + core * (z - y)
    step_p, step_q = 1 + (NZ - 1) * core, NZ - (NZ - 1) * core

    def at_p(d):
        t = lax.rem(p + d, NZ)
        return t, (c, t * step_p + q * step_q)

    def at_q(d):
        t = lax.rem(q + d, NY)
        return t, (c, p * step_p + t * step_q)

    def at_x(d):
        t = lax.rem(x + d, NX)
        return t, (t * 2 + core, w)

    mate = (x * 2 + other, w)

    barrier = pltpu.get_barrier_semaphore()
    greeted = 0
    peers = [at_q(d)[1] for d in range(1, NY)] + [at_p(d)[1] for d in range(1, NZ)]
    finals = []
    for dx in range(NX):
        for dc in range(2):
            tx = lax.rem(x + dx, NX)
            tc = tx * 2 + (core if dc == 0 else other)
            for dp in range(2):
                if dx or dc or dp:
                    finals.append((dx, dc, dp, tc, (tc, partner_w if dp else w)))
                    if dx or dc:
                        peers.append((tc, partner_w if dp else w))
    for peer in peers:
        pl.semaphore_signal(barrier, inc=1, device_id=peer, device_id_type=MESH)
        greeted += 1

    started = []

    def send(src, dst, device):
        i = len(started)
        copy = pltpu.make_async_remote_copy(
            src_ref=src, dst_ref=dst, send_sem=ssem.at[i], recv_sem=rsem.at[i],
            device_id=device, device_id_type=MESH,
        )
        copy.start()
        started.append(copy)
        return copy

    drained = []

    def drain(but=()):
        for copy in started:
            if not any(copy is kept for kept in drained) and not any(copy is kept for kept in but):
                copy.wait_send()
                drained.append(copy)

    load_w = pltpu.make_async_copy(walkers.at[x], wbuf, lsem.at[0])
    load_h = pltpu.make_async_copy(half, hbuf, lsem.at[1])
    load_d = pltpu.make_async_copy(draw, drawbuf, lsem.at[2])
    load_c = [
        pltpu.make_async_copy(
            chol.at[pl.ds(XI * x, XI), :, pl.ds(pl.multiple_of(LH * core + LANES * v, LANES), LANES)],
            cr.at[v, c],
            lsem.at[3 + v],
        )
        for v in range(LH // LANES)
    ]
    load_i = pltpu.make_async_copy(inverse.at[x], ibuf, lsem.at[6])
    load_i.start()
    load_w.start()
    load_h.start()
    load_d.start()
    for copy in load_c:
        copy.start()
    load_all = pltpu.make_async_copy(chol, cbuf, lsem.at[7])
    load_all.start()

    load_w.wait()
    electron = lax.broadcasted_iota(jnp.int32, (LANES, M), 0)
    up = jnp.where(electron < HALF_E, wbuf[0:LANES, :], 0.0)
    down = jnp.where(electron >= SHIFT, wbuf[2 * HALF_E - LANES : 2 * HALF_E, :], 0.0)
    wt[...] = jnp.where(core == 0, up, down).T
    wide = wt[...]
    wide_hi = wide.astype(jnp.bfloat16)
    wide_lo = (wide - wide_hi.astype(jnp.float32)).astype(jnp.bfloat16)
    load_i.wait()
    ipad[...] = jnp.zeros_like(ipad)
    ipad[0:HALF_E, 0:HALF_E] = ibuf[pl.ds(core, HALF_E, stride=2), :]
    inv = ipad[...]
    inv = jnp.where(core == 0, inv, pltpu.roll(pltpu.roll(inv, SHIFT, 0), SHIFT, 1))
    inv_hi = inv.astype(jnp.bfloat16)
    inv_lo = (inv - inv_hi.astype(jnp.float32)).astype(jnp.bfloat16)
    mixed = lax.dot_general(
        jnp.concatenate([wide_hi, wide_lo, wide_hi, wide_lo], axis=1),
        jnp.concatenate([inv_hi, inv_hi, inv_lo, inv_lo], axis=1),
        (((1,), (1,)), ((), ())),
        preferred_element_type=jnp.float32,
    )
    rows_y = M // NY

    @pl.when(core == 0)
    def _():
        m1[...] = mixed.astype(jnp.bfloat16).reshape(NY, rows_y, LANES)

    @pl.when(core == 1)
    def _():
        s1f[...] = mixed

        @pl.loop(0, NZ)
        def _(t):
            for r in range(KW // 2):
                pair = [s1f[pl.ds(KW * t + 2 * r + h, NY, stride=rows_y), :] for h in range(2)]
                m1[t, 16 * r : 16 * (r + 1)] = jnp.concatenate(pair, axis=0).astype(jnp.bfloat16)

    s1[q] = m1[q]

    pl.semaphore_wait(barrier, greeted)

    copies = []
    for d in FAR_FIRST:
        t, device = at_q(d)
        copies.append(send(m1.at[t], s1.at[q], device))

    chol_copies = []

    def send_chol(pieces):
        for dx, dc, v in pieces:
            tx = lax.rem(x + dx, NX)
            tcore = core if dc == 0 else other
            columns = pl.ds(pl.multiple_of(LH * tcore + LANES * v, LANES), LANES)
            copy = send(cbuf.at[pl.ds(XI * tx, XI), :, columns], cr.at[v, c], (tx * 2 + tcore, w))
            chol_copies.append((v, copy))

    load_all.wait()
    send_chol(CHOL_PLAN[0])

    load_h.wait()
    for k in range(KW):
        rows = hbuf[k].astype(jnp.float32)
        first = rows[0:LANES]
        second = rows[2 * HALF_E - LANES : 2 * HALF_E]
        hs[core, LANES * k : LANES * (k + 1)] = jnp.where(core == 0, first, second).astype(jnp.bfloat16)
        hsend[LANES * k : LANES * (k + 1)] = jnp.where(core == 0, second, first).astype(jnp.bfloat16)
    half_copy = send(hsend, hs.at[core], mate)

    row = lax.broadcasted_iota(jnp.int32, (WALKERS, WALKERS), 0)
    column = lax.broadcasted_iota(jnp.int32, (WALKERS, WALKERS), 1)
    target = (row & 7) * (WALKERS // NZ) + (row & 24) + (row >> 5)
    swap[...] = jnp.where(column == target, 1.0, 0.0).astype(jnp.bfloat16)

    load_d.wait()

    @pl.when(core == 0)
    def _():
        for g in range(NX):
            owndraw[8 * g : 8 * (g + 1)] = drawbuf[pl.ds(NX * z + g, NY, stride=NX * NZ), :]

    @pl.when(core == 1)
    def _():
        for g in range(NX):
            owndraw[8 * g : 8 * (g + 1)] = drawbuf[pl.ds(NX * NZ * y + g, NZ, stride=NX), :]

    for copy in copies:
        copy.wait_recv()

    for t in range(NY):
        s1f[rows_y * t : rows_y * (t + 1)] = s1[t].astype(jnp.float32)

    @pl.loop(0, NZ)
    def _(t):
        for r in range(KW // 2):
            pair = []
            for h in range(2):
                first = t * (KW - (KW - 1) * core) + (2 * r + h) * (1 + (NY - 1) * core)
                pair.append(s1f[pl.ds(first, NY, stride=rows_y), :])
            s2[t, 16 * r : 16 * (r + 1)] = jnp.concatenate(pair, axis=0).astype(jnp.bfloat16)

    mx[x, p] = s2[p]
    copies = []
    for d in FAR_FIRST:
        t, device = at_p(d)
        copies.append(send(s2.at[t], mx.at[x, p], device))

    x_copies = []
    for d in (0,) + NEAR_FIRST:
        if d:
            copies[FAR_FIRST.index(d)].wait_recv()
        source = lax.rem(p - d + NZ, NZ)
        for e in (2, 1, 3):
            x_copies.append((d, send(mx.at[x, source], mx.at[x, source], at_x(e)[1])))
    half_copy.wait_recv()

    order = (0,) + NEAR_FIRST
    size = NZ // BIAS_PARTS
    for n in range(BIAS_PARTS):
        group = order[size * n : size * (n + 1)]
        for d in group:
            for offset, copy in x_copies:
                if offset == d:
                    copy.wait_recv()
        for j, d in enumerate(group):
            t = lax.rem(p - d + NZ, NZ)
            for r in range(KW // 2):
                blocks = [mx[g, t, 16 * r : 16 * (r + 1)].astype(jnp.float32) for g in range(NX)]
                for h in range(2):
                    rows = jnp.concatenate([b[8 * h : 8 * (h + 1)] for b in blocks], axis=0)
                    k = 2 * r + h
                    mbig[size * n + j, :, LANES * k : LANES * (k + 1)] = rows.astype(jnp.bfloat16)
        vectors = jnp.concatenate([hs[0], hs[1]], axis=1)
        part = jnp.dot(
            mbig[size * n : size * (n + 1)].reshape(WALKERS // BIAS_PARTS, KW * LANES),
            vectors,
            preferred_element_type=jnp.float32,
        )
        for j, d in enumerate(group):
            t = lax.rem(p - d + NZ, NZ)
            rows = WALKERS // NZ
            biasbuf[t] = part[rows * j : rows * (j + 1)]
    send_chol(CHOL_PLAN[1])
    bias = biasbuf[...].reshape(WALKERS, 2 * GROUP)

    low_part, high_part = bias[:, :GROUP], bias[:, GROUP:]
    theirs = jnp.where(core == 0, high_part, low_part).astype(jnp.bfloat16)
    psend[...] = jnp.dot(swap[...], theirs, preferred_element_type=jnp.float32).astype(jnp.bfloat16)
    spin_copy = send(psend, precv, mate)
    ours = jnp.where(core == 0, low_part, high_part)
    spin_copy.wait_recv()
    both = (ours + precv[...].astype(jnp.float32)).astype(jnp.bfloat16)
    fz[...] = both.reshape(NZ, WALKERS // NZ, GROUP)

    fr[p] = fz[p]
    copies = []
    for d in FAR_FIRST:
        t, device = at_p(d)
        copies.append(send(fz.at[t], fr.at[p], device))
    send_chol(CHOL_PLAN[2])
    for copy in copies:
        copy.wait_recv()
    fy[...] = jnp.sum(fr[...].astype(jnp.float32), axis=0).astype(jnp.bfloat16)
    fyr[q] = fy[...]
    copies = []
    for d in FAR_FIRST:
        t, device = at_q(d)
        copies.append(send(fy, fyr.at[q], device))
    send_chol(CHOL_PLAN[3])
    for copy in copies:
        copy.wait_recv()
    total = jnp.sum(fyr[...].astype(jnp.float32), axis=0)
    sg[c, p] = (owndraw[...] + root_step * total).astype(jnp.bfloat16)

    copies = []
    for d in FAR_FIRST:
        t, device = at_p(d)
        copies.append(send(sg.at[c, p], sg.at[c, p], device))
    send_chol(CHOL_PLAN[4])
    x_copies = []
    for d in (0,) + NEAR_FIRST:
        if d:
            copies[FAR_FIRST.index(d)].wait_recv()
        source = lax.rem(p - d + NZ, NZ)
        for e in (2, 1, 3):
            x_copies.append((e, send(sg.at[c, source], sg.at[c, source], at_x(e)[1])))
    mate_copies = [send(sg.at[c], sg.at[c], mate)]
    for e in (1, 3, 2):
        for offset, copy in x_copies:
            if offset == e:
                copy.wait_recv()
        source = lax.rem(x - e + NX, NX) * 2 + core
        mate_copies.append(send(sg.at[source], sg.at[source], mate))
    for copy in mate_copies:
        copy.wait_recv()
    shifted = jnp.concatenate([sg[2 * g + core].reshape(WALKERS, GROUP) for g in range(NX)], axis=1)
    swapped = jnp.concatenate([sg[2 * g + other].reshape(WALKERS, GROUP) for g in range(NX)], axis=1)
    swapped = jnp.dot(swap[...], swapped, preferred_element_type=jnp.float32).astype(jnp.bfloat16)
    shifted = jnp.concatenate([shifted, swapped], axis=1)
    block = WALKERS // NZ
    run = XI * NY

    def to_p(v):
        load_c[v].wait()
        for chunk, copy in chol_copies:
            if chunk == v:
                copy.wait_recv()
        columns = jnp.concatenate(
            [
                jnp.concatenate([cr[v, 2 * g + h, i] for i in range(XI)], axis=1)
                for h in (core, other)
                for g in range(NX)
            ],
            axis=0,
        )
        product = jnp.dot(shifted, columns, preferred_element_type=jnp.float32)
        product = (root_step * product).astype(jnp.bfloat16)
        for i in range(XI):
            part = product[:, LANES * i : LANES * (i + 1)]
            pz[v, :, block * i : block * (i + 1), :] = part.reshape(NZ, block, LANES)
        rz[v, p] = pz[v, p]
        copies = []
        for d in FAR_FIRST:
            t, device = at_p(d)
            copies.append(send(pz.at[v, t], rz.at[v, p], device))
        return copies

    def to_x(v):
        @pl.loop(0, NZ // 2)
        def _(pair):
            tiles = []
            for t in range(2):
                for i in range(XI):
                    tiles.append(rz[v, 2 * pair + t, block * i : block * (i + 1), :].astype(jnp.float32))
            for r in range(XI):
                for g in range(NX):
                    two = [tiles[2 * r + h][8 * g : 8 * (g + 1)] for h in range(2)]
                    start = pl.multiple_of(2 * run * pair + 16 * r, 16)
                    qx[v, g, pl.ds(start, 16), :] = jnp.concatenate(two, axis=0).astype(jnp.bfloat16)

        rx[v, x] = qx[v, x]
        copies = []
        for d in range(1, NX):
            t, device = at_x(d)
            copies.append(send(qx.at[v, t], rx.at[v, x], device))
        return copies

    def strided(v, put):
        @pl.loop(0, NY)
        def _(t):
            for r in range(rows_y // 16):
                two = [gbuf[v, pl.ds((16 * r + 8 * h) * NY + t, 8, stride=NY), :] for h in range(2)]
                put(t, 16 * r, jnp.concatenate(two, axis=0).astype(jnp.bfloat16))

    def to_q(v):
        @pl.loop(0, NZ // 2)
        def _(pair):
            for g in range(NX):
                rows = rx[v, g, pl.ds(pl.multiple_of(2 * run * pair, 16), 2 * run), :].astype(jnp.float32)
                for t in range(2):
                    for i in range(XI):
                        at = (2 * pair + t) * (KW - (KW - 1) * core) + (XI * g + i) * (1 + (NY - 1) * core)
                        start = pl.multiple_of(NY * at, 8)
                        gbuf[v, pl.ds(start, 8), :] = rows[run * t + 8 * i : run * t + 8 * (i + 1)]

        def put(t, r, rows):
            qy[v, t, r : r + 16, :] = rows

        strided(v, put)
        rb[v, q] = qy[v, q]
        copies = []
        for d in FAR_FIRST:
            t, device = at_q(d)
            copies.append(send(qy.at[v, t], rb.at[v, q], device))
        return copies

    def to_mate(v):
        @pl.when(core == 0)
        def _():
            fb[0, v] = rb[v]

        @pl.when(core == 1)
        def _():
            gbuf[v] = rb[v].astype(jnp.float32).reshape(M, LANES)

            def put(t, r, rows):
                fb[1, v, t, r : r + 16, :] = rows

            strided(v, put)

        return send(fb.at[core, v], fb.at[core, v], mate)

    chunks = LH // LANES
    in_p = [to_p(v) for v in range(chunks)]
    in_x, in_q, in_mate = [], [], []
    drain(sum(in_p, []))
    for v in range(chunks):
        for copy in in_p[v]:
            copy.wait_recv()
        in_x.append(to_x(v))
    for v in range(chunks):
        for copy in in_x[v]:
            copy.wait_recv()
        in_q.append(to_q(v))
    drain(sum(in_q, []))
    for v in range(chunks):
        for copy in in_q[v]:
            copy.wait_recv()
        in_mate.append(to_mate(v))
    drain(in_mate)
    for copy in in_mate:
        copy.wait_recv()

    cur[...] = wt[...].astype(jnp.bfloat16)
    prop[...] = wt[...]
    for degree in range(1, 5):
        field = jnp.concatenate(
            [fb[q, v].reshape(M, LANES) for q in range(2) for v in range(chunks)], axis=1
        )
        term = jnp.dot(field, cur[...], preferred_element_type=jnp.float32)
        if degree > 1:
            term = term / degree
        prop[...] += term
        if degree < 4:
            cur[...] = term.astype(jnp.bfloat16)

    rows_c = M // (2 * NX)
    low[...] = prop[...].astype(jnp.bfloat16)
    copies = []
    own_slot = lax.rem(w, 2) * NX + x
    for dx, dc, dp, tc, device in sorted(finals, key=lambda f: (-f[2], abs(f[0] - 2))):
        start = pl.multiple_of(rows_c * tc, 16)
        copies.append(send(low.at[pl.ds(start, rows_c)], cand.at[own_slot, core], device))
    cand[own_slot, core] = low[pl.ds(pl.multiple_of(rows_c * c, 16), rows_c), :]

    first = lax.div(w, 2) * (2 * NX)
    sums = counts[first]
    source = [jnp.int32(0)] * NX
    for i in range(2 * NX):
        if i:
            sums = sums + counts[first + i]
        for j in range(NX):
            source[j] = source[j] + jnp.where(sums <= lax.rem(w, 2) * NX + j, 1, 0)
    source = [jnp.minimum(s, 2 * NX - 1) for s in source]
    for copy in copies:
        copy.wait_recv()
    lane = lax.broadcasted_iota(jnp.int32, (rows_c, LANES), 1)
    for j in range(NX):
        up = cand[source[j], 0].astype(jnp.float32)
        down = pltpu.roll(cand[source[j], 1].astype(jnp.float32), HALF_E - SHIFT, 1)
        out[j, :, 0:LANES] = jnp.where(lane < HALF_E, up, down)
        out[j, :, LANES : 2 * HALF_E] = down[:, : 2 * HALF_E - LANES]

    drain()


def local(walkers, inv_intersection, half_vectors, chol_vectors, field_draw, counts):
    inverse = inv_intersection.transpose(0, 2, 1, 3).reshape(NX, 2 * HALF_E, HALF_E)
    half = half_vectors.transpose(2, 1, 0)
    chol = chol_vectors.transpose(1, 0, 2)
    f32, bf16 = jnp.float32, jnp.bfloat16
    rows_y, rows_c, block = M // NY, M // (2 * NX), WALKERS // NZ
    chunks = LH // LANES
    vmem = pltpu.VMEM
    scratch = dict(
        wbuf=vmem((2 * HALF_E, M), f32),
        ibuf=vmem((2 * HALF_E, HALF_E), f32),
        ipad=vmem((LANES, LANES), f32),
        wt=vmem((M, LANES), f32),
        hbuf=vmem((KW, 2 * HALF_E, GROUP), bf16),
        hs=vmem((2, KW * LANES, GROUP), bf16),
        hsend=vmem((KW * LANES, GROUP), bf16),
        m1=vmem((NY, rows_y, LANES), bf16),
        s1=vmem((NY, rows_y, LANES), bf16),
        s1f=vmem((NY * rows_y, LANES), f32),
        s2=vmem((NZ, KW * NY, LANES), bf16),
        mx=vmem((NX, NZ, KW * NY, LANES), bf16),
        mbig=vmem((NZ, block, KW * LANES), bf16),
        biasbuf=vmem((NZ, block, 2 * GROUP), f32),
        swap=vmem((WALKERS, WALKERS), bf16),
        psend=vmem((WALKERS, GROUP), bf16),
        precv=vmem((WALKERS, GROUP), bf16),
        fz=vmem((NZ, block, GROUP), bf16),
        fr=vmem((NZ, block, GROUP), bf16),
        fy=vmem((block, GROUP), bf16),
        fyr=vmem((NY, block, GROUP), bf16),
        drawbuf=vmem((WALKERS, GROUP), f32),
        owndraw=vmem((block, GROUP), f32),
        sg=vmem((2 * NX, NZ, block, GROUP), bf16),
        cbuf=vmem((KW, GROUP, M), bf16),
        cr=vmem((chunks, 2 * NX, XI, GROUP, LANES), bf16),
        pz=vmem((chunks, NZ, XI * block, LANES), bf16),
        rz=vmem((chunks, NZ, XI * block, LANES), bf16),
        qx=vmem((chunks, NX, NZ * XI * NY, LANES), bf16),
        rx=vmem((chunks, NX, NZ * XI * NY, LANES), bf16),
        gbuf=vmem((chunks, NZ * NX * XI * NY, LANES), f32),
        qy=vmem((chunks, NY, rows_y, LANES), bf16),
        rb=vmem((chunks, NY, rows_y, LANES), bf16),
        fb=vmem((2, chunks, NY, rows_y, LANES), bf16),
        cur=vmem((M, LANES), bf16),
        prop=vmem((M, LANES), f32),
        low=vmem((M, LANES), bf16),
        cand=vmem((2 * NX, 2, rows_c, LANES), bf16),
        ssem=pltpu.SemaphoreType.DMA((COPIES,)),
        rsem=pltpu.SemaphoreType.DMA((COPIES,)),
        lsem=pltpu.SemaphoreType.DMA((8,)),
    )
    hbm = pl.BlockSpec(memory_space=pltpu.HBM)
    in_vmem = pl.BlockSpec(memory_space=pltpu.VMEM)
    in_smem = pl.BlockSpec(memory_space=pltpu.SMEM)
    operands = [walkers, inverse, half, chol, field_draw, counts]
    operands = [pltpu.with_memory_space_constraint(v, pltpu.HBM) for v in operands]
    result = pl.pallas_call(
        kernel,
        out_shape=jax.ShapeDtypeStruct((NX, rows_c, 2 * HALF_E), f32),
        in_specs=[hbm, hbm, hbm, hbm, hbm, in_smem],
        out_specs=in_vmem,
        scratch_shapes=list(scratch.values()),
        compiler_params=pltpu.CompilerParams(
            collective_id=0, has_side_effects=True, vmem_limit_bytes=48 * 2**20
        ),
    )(*operands)
    return result.transpose(0, 2, 1)


def solution(mesh):
    placed = (
        P("walk", None, None),
        P("walk", None, None, None),
        P("chol", None, "walk"),
        P("chol", "walk", None),
        P(None, "chol"),
        P(),
    )
    return jax.shard_map(
        local, mesh=mesh, in_specs=placed, out_specs=P("walk", None, "chol"), check_vma=False
    )
```

```python
import jax
import jax.numpy as jnp
from jax import lax
from jax.experimental import pallas as pl
from jax.experimental.pallas import tpu as pltpu
from jax.sharding import PartitionSpec as P

root_step = 0.1

NX, NY, NZ = 4, 8, 8
LANES = 128
HALF_E = 100
SHIFT = LANES - HALF_E
M = 768
LH = M // 2
KW = M // (NY * NZ)
XI = KW // NX
WALKERS = NX * NY * NZ
GROUP = 128
COPIES = 256
FAR_FIRST = (4, 3, 5, 2, 6, 1, 7)
NEAR_FIRST = (1, 7, 2, 6, 3, 5, 4)
NEAR = ((1, 0), (3, 0), (1, 1), (3, 1))
FAR = ((2, 0), (2, 1))
MATE = tuple((0, 1, v) for v in range(3))
NEARS = [tuple((dx, dc, v) for dx, dc in NEAR) for v in range(3)]
FARS = [tuple((dx, dc, v) for dx, dc in FAR) for v in range(3)]
CHOL_PLAN = (MATE + NEARS[0] + NEARS[1], FARS[0] + FARS[1], NEARS[2], FARS[2], ())
BIAS_PARTS = 1
MESH = pl.DeviceIdType.MESH


def kernel(
    walkers, inverse, half, chol, draw, counts, out,
    wbuf, ibuf, ipad, wt, hbuf, hs, hsend, m1, s1, s1f, s2, mx, mbig, biasbuf, swap, psend, precv, fz, fr, fy, fyr,
    drawbuf, owndraw, sg, cbuf, cr, pz, rz, qx, rx, gbuf, qy, rb, fb, cur, prop, low, cand, ssem, rsem, lsem,
):
    c = lax.axis_index("chol")
    w = lax.axis_index("walk")
    x = lax.div(c, 2)
    core = lax.rem(c, 2)
    y = lax.div(w, NZ)
    z = lax.rem(w, NZ)
    other = 1 - core
    partner_w = w + 1 - 2 * lax.rem(w, 2)

    p = z + core * (y - z)
    q = y + core * (z - y)
    step_p, step_q = 1 + (NZ - 1) * core, NZ - (NZ - 1) * core

    def at_p(d):
        t = lax.rem(p + d, NZ)
        return t, (c, t * step_p + q * step_q)

    def at_q(d):
        t = lax.rem(q + d, NY)
        return t, (c, p * step_p + t * step_q)

    def at_x(d):
        t = lax.rem(x + d, NX)
        return t, (t * 2 + core, w)

    mate = (x * 2 + other, w)

    barrier = pltpu.get_barrier_semaphore()
    greeted = 0
    peers = [at_q(d)[1] for d in range(1, NY)] + [at_p(d)[1] for d in range(1, NZ)]
    finals = []
    for dx in range(NX):
        for dc in range(2):
            tx = lax.rem(x + dx, NX)
            tc = tx * 2 + (core if dc == 0 else other)
            for dp in range(2):
                if dx or dc or dp:
                    finals.append((dx, dc, dp, tc, (tc, partner_w if dp else w)))
                    if dx or dc:
                        peers.append((tc, partner_w if dp else w))
    for peer in peers:
        pl.semaphore_signal(barrier, inc=1, device_id=peer, device_id_type=MESH)
        greeted += 1

    started = []

    def send(src, dst, device):
        i = len(started)
        copy = pltpu.make_async_remote_copy(
            src_ref=src, dst_ref=dst, send_sem=ssem.at[i], recv_sem=rsem.at[i],
            device_id=device, device_id_type=MESH,
        )
        copy.start()
        started.append(copy)
        return copy

    drained = []

    def drain(but=()):
        for copy in started:
            if not any(copy is kept for kept in drained) and not any(copy is kept for kept in but):
                copy.wait_send()
                drained.append(copy)

    load_w = pltpu.make_async_copy(walkers.at[x], wbuf, lsem.at[0])
    load_h = pltpu.make_async_copy(half, hbuf, lsem.at[1])
    load_d = pltpu.make_async_copy(draw, drawbuf, lsem.at[2])
    load_c = [
        pltpu.make_async_copy(
            chol.at[pl.ds(XI * x, XI), :, pl.ds(pl.multiple_of(LH * core + LANES * v, LANES), LANES)],
            cr.at[v, c],
            lsem.at[3 + v],
        )
        for v in range(LH // LANES)
    ]
    load_i = pltpu.make_async_copy(inverse.at[x], ibuf, lsem.at[6])
    load_i.start()
    load_w.start()
    load_h.start()
    load_d.start()
    for copy in load_c:
        copy.start()
    load_all = pltpu.make_async_copy(chol, cbuf, lsem.at[7])
    load_all.start()

    load_w.wait()
    electron = lax.broadcasted_iota(jnp.int32, (LANES, M), 0)
    up = jnp.where(electron < HALF_E, wbuf[0:LANES, :], 0.0)
    down = jnp.where(electron >= SHIFT, wbuf[2 * HALF_E - LANES : 2 * HALF_E, :], 0.0)
    wt[...] = jnp.where(core == 0, up, down).T
    wide = wt[...]
    wide_hi = wide.astype(jnp.bfloat16)
    wide_lo = (wide - wide_hi.astype(jnp.float32)).astype(jnp.bfloat16)
    load_i.wait()
    ipad[...] = jnp.zeros_like(ipad)
    ipad[0:HALF_E, 0:HALF_E] = ibuf[pl.ds(core, HALF_E, stride=2), :]
    inv = ipad[...]
    inv = jnp.where(core == 0, inv, pltpu.roll(pltpu.roll(inv, SHIFT, 0), SHIFT, 1))
    inv_hi = inv.astype(jnp.bfloat16)
    inv_lo = (inv - inv_hi.astype(jnp.float32)).astype(jnp.bfloat16)
    mixed = lax.dot_general(
        jnp.concatenate([wide_hi, wide_lo, wide_hi, wide_lo], axis=1),
        jnp.concatenate([inv_hi, inv_hi, inv_lo, inv_lo], axis=1),
        (((1,), (1,)), ((), ())),
        preferred_element_type=jnp.float32,
    )
    rows_y = M // NY

    @pl.when(core == 0)
    def _():
        m1[...] = mixed.astype(jnp.bfloat16).reshape(NY, rows_y, LANES)

    @pl.when(core == 1)
    def _():
        s1f[...] = mixed

        @pl.loop(0, NZ)
        def _(t):
            for r in range(KW // 2):
                pair = [s1f[pl.ds(KW * t + 2 * r + h, NY, stride=rows_y), :] for h in range(2)]
                m1[t, 16 * r : 16 * (r + 1)] = jnp.concatenate(pair, axis=0).astype(jnp.bfloat16)

    s1[q] = m1[q]

    pl.semaphore_wait(barrier, greeted)

    copies = []
    for d in FAR_FIRST:
        t, device = at_q(d)
        copies.append(send(m1.at[t], s1.at[q], device))

    chol_copies = []

    def send_chol(pieces):
        for dx, dc, v in pieces:
            tx = lax.rem(x + dx, NX)
            tcore = core if dc == 0 else other
            columns = pl.ds(pl.multiple_of(LH * tcore + LANES * v, LANES), LANES)
            copy = send(cbuf.at[pl.ds(XI * tx, XI), :, columns], cr.at[v, c], (tx * 2 + tcore, w))
            chol_copies.append((v, copy))

    load_all.wait()
    send_chol(CHOL_PLAN[0])

    load_h.wait()
    for k in range(KW):
        rows = hbuf[k].astype(jnp.float32)
        first = rows[0:LANES]
        second = rows[2 * HALF_E - LANES : 2 * HALF_E]
        hs[core, LANES * k : LANES * (k + 1)] = jnp.where(core == 0, first, second).astype(jnp.bfloat16)
        hsend[LANES * k : LANES * (k + 1)] = jnp.where(core == 0, second, first).astype(jnp.bfloat16)
    half_copy = send(hsend, hs.at[core], mate)

    row = lax.broadcasted_iota(jnp.int32, (WALKERS, WALKERS), 0)
    column = lax.broadcasted_iota(jnp.int32, (WALKERS, WALKERS), 1)
    target = (row & 7) * (WALKERS // NZ) + (row & 24) + (row >> 5)
    swap[...] = jnp.where(column == target, 1.0, 0.0).astype(jnp.bfloat16)

    load_d.wait()

    @pl.when(core == 0)
    def _():
        for g in range(NX):
            owndraw[8 * g : 8 * (g + 1)] = drawbuf[pl.ds(NX * z + g, NY, stride=NX * NZ), :]

    @pl.when(core == 1)
    def _():
        for g in range(NX):
            owndraw[8 * g : 8 * (g + 1)] = drawbuf[pl.ds(NX * NZ * y + g, NZ, stride=NX), :]

    for copy in copies:
        copy.wait_recv()

    for t in range(NY):
        s1f[rows_y * t : rows_y * (t + 1)] = s1[t].astype(jnp.float32)

    @pl.loop(0, NZ)
    def _(t):
        for r in range(KW // 2):
            pair = []
            for h in range(2):
                first = t * (KW - (KW - 1) * core) + (2 * r + h) * (1 + (NY - 1) * core)
                pair.append(s1f[pl.ds(first, NY, stride=rows_y), :])
            s2[t, 16 * r : 16 * (r + 1)] = jnp.concatenate(pair, axis=0).astype(jnp.bfloat16)

    mx[x, p] = s2[p]
    copies = []
    for d in FAR_FIRST:
        t, device = at_p(d)
        copies.append(send(s2.at[t], mx.at[x, p], device))

    x_copies = []
    for d in (0,) + NEAR_FIRST:
        if d:
            copies[FAR_FIRST.index(d)].wait_recv()
        source = lax.rem(p - d + NZ, NZ)
        for e in (2, 1, 3):
            x_copies.append((d, send(mx.at[x, source], mx.at[x, source], at_x(e)[1])))
    half_copy.wait_recv()

    order = (0,) + NEAR_FIRST
    size = NZ // BIAS_PARTS
    for n in range(BIAS_PARTS):
        group = order[size * n : size * (n + 1)]
        for d in group:
            for offset, copy in x_copies:
                if offset == d:
                    copy.wait_recv()
        for j, d in enumerate(group):
            t = lax.rem(p - d + NZ, NZ)
            for r in range(KW // 2):
                blocks = [mx[g, t, 16 * r : 16 * (r + 1)].astype(jnp.float32) for g in range(NX)]
                for h in range(2):
                    rows = jnp.concatenate([b[8 * h : 8 * (h + 1)] for b in blocks], axis=0)
                    k = 2 * r + h
                    mbig[size * n + j, :, LANES * k : LANES * (k + 1)] = rows.astype(jnp.bfloat16)
        vectors = jnp.concatenate([hs[0], hs[1]], axis=1)
        part = jnp.dot(
            mbig[size * n : size * (n + 1)].reshape(WALKERS // BIAS_PARTS, KW * LANES),
            vectors,
            preferred_element_type=jnp.float32,
        )
        for j, d in enumerate(group):
            t = lax.rem(p - d + NZ, NZ)
            rows = WALKERS // NZ
            biasbuf[t] = part[rows * j : rows * (j + 1)]
    send_chol(CHOL_PLAN[1])
    bias = biasbuf[...].reshape(WALKERS, 2 * GROUP)

    low_part, high_part = bias[:, :GROUP], bias[:, GROUP:]
    theirs = jnp.where(core == 0, high_part, low_part).astype(jnp.bfloat16)
    psend[...] = jnp.dot(swap[...], theirs, preferred_element_type=jnp.float32).astype(jnp.bfloat16)
    spin_copy = send(psend, precv, mate)
    ours = jnp.where(core == 0, low_part, high_part)
    spin_copy.wait_recv()
    both = (ours + precv[...].astype(jnp.float32)).astype(jnp.bfloat16)
    fz[...] = both.reshape(NZ, WALKERS // NZ, GROUP)

    fr[p] = fz[p]
    copies = []
    for d in FAR_FIRST:
        t, device = at_p(d)
        copies.append(send(fz.at[t], fr.at[p], device))
    send_chol(CHOL_PLAN[2])
    for copy in copies:
        copy.wait_recv()
    fy[...] = jnp.sum(fr[...].astype(jnp.float32), axis=0).astype(jnp.bfloat16)
    fyr[q] = fy[...]
    copies = []
    for d in FAR_FIRST:
        t, device = at_q(d)
        copies.append(send(fy, fyr.at[q], device))
    send_chol(CHOL_PLAN[3])
    for copy in copies:
        copy.wait_recv()
    total = jnp.sum(fyr[...].astype(jnp.float32), axis=0)
    sg[c, p] = (owndraw[...] + root_step * total).astype(jnp.bfloat16)

    copies = []
    for d in FAR_FIRST:
        t, device = at_p(d)
        copies.append(send(sg.at[c, p], sg.at[c, p], device))
    send_chol(CHOL_PLAN[4])
    x_copies = []
    for d in (0,) + NEAR_FIRST:
        if d:
            copies[FAR_FIRST.index(d)].wait_recv()
        source = lax.rem(p - d + NZ, NZ)
        for e in (2, 1, 3):
            x_copies.append((e, send(sg.at[c, source], sg.at[c, source], at_x(e)[1])))
    mate_copies = [send(sg.at[c], sg.at[c], mate)]
    for e in (1, 3, 2):
        for offset, copy in x_copies:
            if offset == e:
                copy.wait_recv()
        source = lax.rem(x - e + NX, NX) * 2 + core
        mate_copies.append(send(sg.at[source], sg.at[source], mate))
    for copy in mate_copies:
        copy.wait_recv()
    shifted = jnp.concatenate([sg[2 * g + core].reshape(WALKERS, GROUP) for g in range(NX)], axis=1)
    swapped = jnp.concatenate([sg[2 * g + other].reshape(WALKERS, GROUP) for g in range(NX)], axis=1)
    swapped = jnp.dot(swap[...], swapped, preferred_element_type=jnp.float32).astype(jnp.bfloat16)
    shifted = jnp.concatenate([shifted, swapped], axis=1)
    block = WALKERS // NZ
    run = XI * NY

    def to_p(v):
        load_c[v].wait()
        for chunk, copy in chol_copies:
            if chunk == v:
                copy.wait_recv()
        columns = jnp.concatenate(
            [
                jnp.concatenate([cr[v, 2 * g + h, i] for i in range(XI)], axis=1)
                for h in (core, other)
                for g in range(NX)
            ],
            axis=0,
        )
        product = jnp.dot(shifted, columns, preferred_element_type=jnp.float32)
        product = (root_step * product).astype(jnp.bfloat16)
        for i in range(XI):
            part = product[:, LANES * i : LANES * (i + 1)]
            pz[v, :, block * i : block * (i + 1), :] = part.reshape(NZ, block, LANES)
        rz[v, p] = pz[v, p]
        copies = []
        for d in FAR_FIRST:
            t, device = at_p(d)
            copies.append(send(pz.at[v, t], rz.at[v, p], device))
        return copies

    def to_x(v):
        @pl.loop(0, NZ // 2)
        def _(pair):
            tiles = []
            for t in range(2):
                for i in range(XI):
                    tiles.append(rz[v, 2 * pair + t, block * i : block * (i + 1), :].astype(jnp.float32))
            for r in range(XI):
                for g in range(NX):
                    two = [tiles[2 * r + h][8 * g : 8 * (g + 1)] for h in range(2)]
                    start = pl.multiple_of(2 * run * pair + 16 * r, 16)
                    qx[v, g, pl.ds(start, 16), :] = jnp.concatenate(two, axis=0).astype(jnp.bfloat16)

        rx[v, x] = qx[v, x]
        copies = []
        for d in (2, 1, 3):
            t, device = at_x(d)
            copies.append(send(qx.at[v, t], rx.at[v, x], device))
        return copies

    def strided(v, put):
        @pl.loop(0, NY)
        def _(t):
            for r in range(rows_y // 16):
                two = [gbuf[v, pl.ds((16 * r + 8 * h) * NY + t, 8, stride=NY), :] for h in range(2)]
                put(t, 16 * r, jnp.concatenate(two, axis=0).astype(jnp.bfloat16))

    def to_q(v):
        @pl.loop(0, NZ // 2)
        def _(pair):
            for g in range(NX):
                rows = rx[v, g, pl.ds(pl.multiple_of(2 * run * pair, 16), 2 * run), :].astype(jnp.float32)
                for t in range(2):
                    for i in range(XI):
                        at = (2 * pair + t) * (KW - (KW - 1) * core) + (XI * g + i) * (1 + (NY - 1) * core)
                        start = pl.multiple_of(NY * at, 8)
                        gbuf[v, pl.ds(start, 8), :] = rows[run * t + 8 * i : run * t + 8 * (i + 1)]

        def put(t, r, rows):
            qy[v, t, r : r + 16, :] = rows

        strided(v, put)
        rb[v, q] = qy[v, q]
        copies = []
        for d in FAR_FIRST:
            t, device = at_q(d)
            copies.append(send(qy.at[v, t], rb.at[v, q], device))
        return copies

    def to_mate(v):
        @pl.when(core == 0)
        def _():
            fb[0, v] = rb[v]

        @pl.when(core == 1)
        def _():
            gbuf[v] = rb[v].astype(jnp.float32).reshape(M, LANES)

            def put(t, r, rows):
                fb[1, v, t, r : r + 16, :] = rows

            strided(v, put)

        return send(fb.at[core, v], fb.at[core, v], mate)

    chunks = LH // LANES
    in_p = [to_p(v) for v in range(chunks)]
    in_x, in_q, in_mate = [], [], []
    drain(sum(in_p, []))
    for v in range(chunks):
        for copy in in_p[v]:
            copy.wait_recv()
        in_x.append(to_x(v))
    for v in range(chunks):
        for copy in in_x[v]:
            copy.wait_recv()
        in_q.append(to_q(v))
    drain(sum(in_q, []))
    for v in range(chunks):
        for copy in in_q[v]:
            copy.wait_recv()
        in_mate.append(to_mate(v))
    drain(in_mate)
    for copy in in_mate:
        copy.wait_recv()

    cur[...] = wt[...].astype(jnp.bfloat16)
    prop[...] = wt[...]
    for degree in range(1, 5):
        field = jnp.concatenate(
            [fb[q, v].reshape(M, LANES) for q in range(2) for v in range(chunks)], axis=1
        )
        term = jnp.dot(field, cur[...], preferred_element_type=jnp.float32)
        if degree > 1:
            term = term / degree
        prop[...] += term
        if degree < 4:
            cur[...] = term.astype(jnp.bfloat16)

    rows_c = M // (2 * NX)
    low[...] = prop[...].astype(jnp.bfloat16)
    copies = []
    own_slot = lax.rem(w, 2) * NX + x
    for dx, dc, dp, tc, device in sorted(finals, key=lambda f: (-f[2], abs(f[0] - 2))):
        start = pl.multiple_of(rows_c * tc, 16)
        copies.append(send(low.at[pl.ds(start, rows_c)], cand.at[own_slot, core], device))
    cand[own_slot, core] = low[pl.ds(pl.multiple_of(rows_c * c, 16), rows_c), :]

    first = lax.div(w, 2) * (2 * NX)
    sums = counts[first]
    source = [jnp.int32(0)] * NX
    for i in range(2 * NX):
        if i:
            sums = sums + counts[first + i]
        for j in range(NX):
            source[j] = source[j] + jnp.where(sums <= lax.rem(w, 2) * NX + j, 1, 0)
    source = [jnp.minimum(s, 2 * NX - 1) for s in source]
    for copy in copies:
        copy.wait_recv()
    lane = lax.broadcasted_iota(jnp.int32, (rows_c, LANES), 1)
    for j in range(NX):
        up = cand[source[j], 0].astype(jnp.float32)
        down = pltpu.roll(cand[source[j], 1].astype(jnp.float32), HALF_E - SHIFT, 1)
        out[j, :, 0:LANES] = jnp.where(lane < HALF_E, up, down)
        out[j, :, LANES : 2 * HALF_E] = down[:, : 2 * HALF_E - LANES]

    drain()


def local(walkers, inv_intersection, half_vectors, chol_vectors, field_draw, counts):
    inverse = inv_intersection.transpose(0, 2, 1, 3).reshape(NX, 2 * HALF_E, HALF_E)
    half = half_vectors.transpose(2, 1, 0)
    chol = chol_vectors.transpose(1, 0, 2)
    f32, bf16 = jnp.float32, jnp.bfloat16
    rows_y, rows_c, block = M // NY, M // (2 * NX), WALKERS // NZ
    chunks = LH // LANES
    vmem = pltpu.VMEM
    scratch = dict(
        wbuf=vmem((2 * HALF_E, M), f32),
        ibuf=vmem((2 * HALF_E, HALF_E), f32),
        ipad=vmem((LANES, LANES), f32),
        wt=vmem((M, LANES), f32),
        hbuf=vmem((KW, 2 * HALF_E, GROUP), bf16),
        hs=vmem((2, KW * LANES, GROUP), bf16),
        hsend=vmem((KW * LANES, GROUP), bf16),
        m1=vmem((NY, rows_y, LANES), bf16),
        s1=vmem((NY, rows_y, LANES), bf16),
        s1f=vmem((NY * rows_y, LANES), f32),
        s2=vmem((NZ, KW * NY, LANES), bf16),
        mx=vmem((NX, NZ, KW * NY, LANES), bf16),
        mbig=vmem((NZ, block, KW * LANES), bf16),
        biasbuf=vmem((NZ, block, 2 * GROUP), f32),
        swap=vmem((WALKERS, WALKERS), bf16),
        psend=vmem((WALKERS, GROUP), bf16),
        precv=vmem((WALKERS, GROUP), bf16),
        fz=vmem((NZ, block, GROUP), bf16),
        fr=vmem((NZ, block, GROUP), bf16),
        fy=vmem((block, GROUP), bf16),
        fyr=vmem((NY, block, GROUP), bf16),
        drawbuf=vmem((WALKERS, GROUP), f32),
        owndraw=vmem((block, GROUP), f32),
        sg=vmem((2 * NX, NZ, block, GROUP), bf16),
        cbuf=vmem((KW, GROUP, M), bf16),
        cr=vmem((chunks, 2 * NX, XI, GROUP, LANES), bf16),
        pz=vmem((chunks, NZ, XI * block, LANES), bf16),
        rz=vmem((chunks, NZ, XI * block, LANES), bf16),
        qx=vmem((chunks, NX, NZ * XI * NY, LANES), bf16),
        rx=vmem((chunks, NX, NZ * XI * NY, LANES), bf16),
        gbuf=vmem((chunks, NZ * NX * XI * NY, LANES), f32),
        qy=vmem((chunks, NY, rows_y, LANES), bf16),
        rb=vmem((chunks, NY, rows_y, LANES), bf16),
        fb=vmem((2, chunks, NY, rows_y, LANES), bf16),
        cur=vmem((M, LANES), bf16),
        prop=vmem((M, LANES), f32),
        low=vmem((M, LANES), bf16),
        cand=vmem((2 * NX, 2, rows_c, LANES), bf16),
        ssem=pltpu.SemaphoreType.DMA((COPIES,)),
        rsem=pltpu.SemaphoreType.DMA((COPIES,)),
        lsem=pltpu.SemaphoreType.DMA((8,)),
    )
    hbm = pl.BlockSpec(memory_space=pltpu.HBM)
    in_vmem = pl.BlockSpec(memory_space=pltpu.VMEM)
    in_smem = pl.BlockSpec(memory_space=pltpu.SMEM)
    operands = [walkers, inverse, half, chol, field_draw, counts]
    operands = [pltpu.with_memory_space_constraint(v, pltpu.HBM) for v in operands]
    result = pl.pallas_call(
        kernel,
        out_shape=jax.ShapeDtypeStruct((NX, rows_c, 2 * HALF_E), f32),
        in_specs=[hbm, hbm, hbm, hbm, hbm, in_smem],
        out_specs=in_vmem,
        scratch_shapes=list(scratch.values()),
        compiler_params=pltpu.CompilerParams(
            collective_id=0, has_side_effects=True, vmem_limit_bytes=48 * 2**20
        ),
    )(*operands)
    return result.transpose(0, 2, 1)


def solution(mesh):
    placed = (
        P("walk", None, None),
        P("walk", None, None, None),
        P("chol", None, "walk"),
        P("chol", "walk", None),
        P(None, "chol"),
        P(),
    )
    return jax.shard_map(
        local, mesh=mesh, in_specs=placed, out_specs=P("walk", None, "chol"), check_vma=False
    )
```
